256 devices in a mesh: replica: 64 (over y, x_hi, z), mp: 4 (over x_lo, core).
Axes of the slice: x: 4 (x_hi: 2, x_lo: 2; x = x_hi * 2 + x_lo), y: 4, z: 8, core: 2. Of those that a mesh axis runs over, the one named last changes fastest.
Arguments:
- local_weights: bfloat16 [64, 4, 16, 16384], P('replica', None, None, 'mp')
- outer_weights: float32 [4, 16, 16384], P(None, None, 'mp')
- momentum: float32 [4, 16, 16384], P(None, None, 'mp'), may hold values from -1.8 to 1.8
- plan: int32 [4], replicated, may hold values from 0 to 3, each once
Outputs:
- new_outer: float32 [2, 16, 16384], P(None, None, 'mp')
- new_moment: float32 [2, 16, 16384], P(None, None, 'mp')
- merged: bfloat16 [64, 2, 16, 16384], P('replica', None, None, 'mp')
The draws below stay inside these ranges and needn't reach their ends.
Inputs may be any that keep to these rules, and one draw needn't show every extreme that they name: `plan`: each fragment number appears once; the first 2 entries name the fragments synchronized now.
All inputs are finite; a program needn't handle non-finite values. Where the reference program divides by a largest or mean magnitude, that divisor is 1e-20 or more.
Results may differ from the reference program's by a relative error of at most 0.001.
Values sent between devices are 32-bit elements; how exact they have to be, the bound alone decides.
No kernel may reach another device: no remote copies, remote signals or barrier semaphores. Data moves between devices by JAX's collectives and lax.ppermute only.
A program may use at most 192 MiB of HBM per device.

```python
import jax
import jax.numpy as jnp
from jax import lax

FF = 16384
ROWS = 16
FRAGS = 4
SYNCED = 2
BLOCK = 128
REPLICAS = 64


def shared_parts(key):
    outer = jax.random.normal(jax.random.fold_in(key, 11), (FRAGS, ROWS, FF), jnp.float32)
    row_scale = 10.0 ** (0.5 * jax.random.uniform(jax.random.fold_in(key, 12), (FRAGS, ROWS, 1), jnp.float32))
    position = jnp.arange(FF, dtype=jnp.float32) / FF
    col_scale = 10.0 ** (0.5 * position) * jax.random.uniform(jax.random.fold_in(key, 13), (FF,), jnp.float32, 0.6, 1.4)
    common = jax.random.normal(jax.random.fold_in(key, 14), (FRAGS, ROWS, FF), jnp.float32)
    return (outer, row_scale * col_scale, common)


def draw_outer_weights(key, part):
    outer, spread, common = shared_parts(key)
    return outer


def draw_local_weights(key, part):
    outer, spread, common = shared_parts(key)
    key = jax.random.fold_in(key, 2)
    noise = jax.random.normal(key, (REPLICAS, FRAGS, ROWS, FF), jnp.float32)
    amount = 0.15
    local = outer[None] - amount * spread[None] * (common[None] + noise)
    return local.astype(jnp.bfloat16)


def levels(own_key, extent, cuts, low, top_value):
    factor_of, own = 1.0, jax.random.fold_in(own_key, 6)
    for dim, blocks in cuts:
        heights = jnp.exp(jax.random.uniform(jax.random.fold_in(own, dim), (blocks,), jnp.float32, low / len(cuts), top_value / len(cuts)))
        factor_of = factor_of * jnp.repeat(heights, extent[dim] // blocks).reshape([-1 if axis == dim else 1 for axis in range(len(extent))])
    return factor_of


def bell_draw(key, dims, deviation, limit, pieces=(), kind=jnp.bfloat16):
    result = jax.random.normal(key, dims, jnp.float32) * deviation
    if len(pieces) > 0:
        result = levels(key, dims, pieces, -0.22, 0.18) * result
    return jnp.clip(result, min=-limit, max=limit).astype(kind)


def setup_inputs(seed: int = 0) -> dict:
    key_list = jax.random.split(jax.random.key(seed), 5)
    local_weights = draw_local_weights(jax.random.fold_in(key_list[4], 71), 0)
    outer_weights = draw_outer_weights(jax.random.fold_in(key_list[4], 71), 0)
    momentum = bell_draw(key_list[2], (FRAGS, ROWS, FF), 0.3, 1.8, ((2, 4),), jnp.float32)
    plan = jax.random.permutation(key_list[3], FRAGS).astype(jnp.int32)
    return dict(local_weights=local_weights, outer_weights=outer_weights, momentum=momentum, plan=plan)


EPS = 1e-06
CLIP = 0.2
MU = 0.9
LR = 0.7
MIX = 0.5

def dequantized(diff):
    shape = diff.shape
    blocks = diff.reshape(shape[:-1] + (shape[-1] // BLOCK, BLOCK))
    scale = lax.optimization_barrier(jnp.max(jnp.abs(blocks), axis=-1, keepdims=True)) + EPS
    coded = lax.optimization_barrier((blocks / scale).astype(jnp.bfloat16))
    return (coded.astype(jnp.float32) * scale).reshape(shape)

def reference(local_weights, outer_weights, momentum, plan):
    chosen = plan[:SYNCED].astype(jnp.int32)
    outer_sel = jnp.take(outer_weights, chosen, axis=0)
    moment_sel = jnp.take(momentum, chosen, axis=0)

    def add_one(worker, total):
        local_one = lax.dynamic_index_in_dim(local_weights, worker, 0, keepdims=False)
        local_one = jnp.take(local_one, chosen, axis=0)
        return total + dequantized(outer_sel - local_one.astype(jnp.float32))
    total = lax.fori_loop(0, REPLICAS, add_one, jnp.zeros(outer_sel.shape, jnp.float32))
    pseudo = total / REPLICAS
    meansq = lax.optimization_barrier(jnp.mean(pseudo * pseudo, axis=(1, 2), keepdims=True))
    factor = jnp.minimum(1.0, CLIP / jnp.sqrt(meansq + EPS))
    grad = pseudo * factor
    new_moment = MU * moment_sel + grad
    new_outer = outer_sel - LR * (MU * new_moment + grad)
    local_sel = jnp.take(local_weights, chosen, axis=1)
    merged = (MIX * local_sel.astype(jnp.float32) + (1.0 - MIX) * new_outer[None]).astype(jnp.bfloat16)
    return (new_outer, new_moment, merged)
```

```python
import jax
import jax.numpy as jnp
from jax import lax
from jax.experimental import pallas as pl
from jax.experimental.pallas import tpu as pltpu
from jax.sharding import PartitionSpec as P

SYNCED = 2
BLOCK = 128
EPS = 1e-06
CLIP = 0.2
MU = 0.9
LR = 0.7
MIX = 0.5
VMEM = 40 * 1024 * 1024


def encode_kernel(plan_ref, local_ref, outer_ref, out_ref):
    for b in range(out_ref.shape[0]):
        cols = slice(b * BLOCK, (b + 1) * BLOCK)
        diff = outer_ref[0, :, cols] - local_ref[0, 0, :, cols].astype(jnp.float32)
        scale = jnp.max(jnp.abs(diff), axis=-1, keepdims=True) + EPS
        out_ref[b] = (diff / scale).astype(jnp.bfloat16).astype(jnp.float32) * scale


def encode(plan, local, outer):
    _, frags, rows, cols = local.shape
    blocks = cols // BLOCK
    return pl.pallas_call(
        encode_kernel,
        out_shape=jax.ShapeDtypeStruct((SYNCED * blocks, rows, BLOCK), jnp.float32),
        grid_spec=pltpu.PrefetchScalarGridSpec(
            num_scalar_prefetch=1,
            grid=(SYNCED,),
            in_specs=[
                pl.BlockSpec((1, 1, rows, cols), lambda i, plan: (0, plan[i], 0, 0)),
                pl.BlockSpec((1, rows, cols), lambda i, plan: (plan[i], 0, 0)),
            ],
            out_specs=pl.BlockSpec((blocks, rows, BLOCK), lambda i, plan: (i, 0, 0)),
        ),
        compiler_params=pltpu.CompilerParams(vmem_limit_bytes=VMEM),
        name="encode",
    )(plan, local, outer)


def add_kernel(workers, parts_ref, out_ref):
    total = jnp.sum(parts_ref[...], axis=0) / workers
    out_ref[...] = jnp.broadcast_to(total[None], out_ref.shape)


def add(parts, workers):
    return pl.pallas_call(
        lambda parts_ref, out_ref: add_kernel(workers, parts_ref, out_ref),
        out_shape=jax.ShapeDtypeStruct(parts.shape, jnp.float32),
        compiler_params=pltpu.CompilerParams(vmem_limit_bytes=VMEM),
        name="add",
    )(parts)


def squares_kernel(pseudo_ref, out_ref):
    half = pseudo_ref.shape[0] // SYNCED
    out_ref[...] = jnp.zeros_like(out_ref)
    for f in range(SYNCED):
        part = pseudo_ref[f * half : (f + 1) * half]
        out_ref[f : f + 1] = jnp.broadcast_to(jnp.sum(part * part), (1, BLOCK))


def squares(pseudo):
    return pl.pallas_call(
        squares_kernel,
        out_shape=jax.ShapeDtypeStruct((8, BLOCK), jnp.float32),
        compiler_params=pltpu.CompilerParams(vmem_limit_bytes=VMEM),
        name="squares",
    )(pseudo)


def update_kernel(entries, plan_ref, pseudo_ref, squares_ref, local_ref, outer_ref, moment_ref, new_outer_ref, new_moment_ref, merged_ref):
    f = pl.program_id(0)
    mean = squares_ref[pl.ds(f, 1)] / entries
    factor = jnp.minimum(1.0, CLIP / jnp.sqrt(mean + EPS))
    for b in range(pseudo_ref.shape[0]):
        cols = slice(b * BLOCK, (b + 1) * BLOCK)
        grad = pseudo_ref[b] * factor
        outer = outer_ref[0, :, cols]
        moment_next = MU * moment_ref[0, :, cols] + grad
        outer_next = outer - LR * (MU * moment_next + grad)
        new_moment_ref[0, :, cols] = moment_next
        new_outer_ref[0, :, cols] = outer_next
        local = local_ref[0, 0, :, cols].astype(jnp.float32)
        merged_ref[0, 0, :, cols] = (MIX * local + (1.0 - MIX) * outer_next).astype(jnp.bfloat16)


def update(plan, pseudo, squares_sum, local, outer, moment, entries):
    _, frags, rows, cols = local.shape
    blocks = cols // BLOCK
    chosen = pl.BlockSpec((1, rows, cols), lambda i, plan: (plan[i], 0, 0))
    placed = pl.BlockSpec((1, rows, cols), lambda i, plan: (i, 0, 0))
    return pl.pallas_call(
        lambda *refs: update_kernel(entries, *refs),
        out_shape=(
            jax.ShapeDtypeStruct((SYNCED, rows, cols), jnp.float32),
            jax.ShapeDtypeStruct((SYNCED, rows, cols), jnp.float32),
            jax.ShapeDtypeStruct((1, SYNCED, rows, cols), jnp.bfloat16),
        ),
        grid_spec=pltpu.PrefetchScalarGridSpec(
            num_scalar_prefetch=1,
            grid=(SYNCED,),
            in_specs=[
                pl.BlockSpec((blocks, rows, BLOCK), lambda i, plan: (i, 0, 0)),
                pl.BlockSpec((8, BLOCK), lambda i, plan: (0, 0)),
                pl.BlockSpec((1, 1, rows, cols), lambda i, plan: (0, plan[i], 0, 0)),
                chosen,
                chosen,
            ],
            out_specs=[
                placed,
                placed,
                pl.BlockSpec((1, 1, rows, cols), lambda i, plan: (0, i, 0, 0)),
            ],
        ),
        compiler_params=pltpu.CompilerParams(vmem_limit_bytes=VMEM),
        name="update",
    )(plan, pseudo, squares_sum, local, outer, moment)


def shards(local, outer, moment, plan):
    _, frags, rows, cols = local.shape
    workers = lax.axis_size("replica")
    entries = rows * cols * lax.axis_size("mp")
    pieces = encode(plan, local, outer)
    per_worker = pieces.shape[0] // workers
    parts = lax.all_to_all(pieces, "replica", 0, 0, tiled=True)
    means = add(parts, workers)
    pseudo = lax.all_to_all(means, "replica", 0, 0, tiled=True)
    squares_sum = lax.psum(squares(pseudo), "mp")
    return update(plan, pseudo, squares_sum, local, outer, moment, entries)


def solution(mesh):
    return jax.shard_map(
        shards,
        mesh=mesh,
        in_specs=(P("replica", None, None, "mp"), P(None, None, "mp"), P(None, None, "mp"), P()),
        out_specs=(P(None, None, "mp"), P(None, None, "mp"), P("replica", None, None, "mp")),
        check_vma=False,
    )
```

```python
import jax
import jax.numpy as jnp
from jax import lax
from jax.experimental import pallas as pl
from jax.experimental.pallas import tpu as pltpu
from jax.sharding import PartitionSpec as P

SYNCED = 2
BLOCK = 128
EPS = 1e-06
CLIP = 0.2
MU = 0.9
LR = 0.7
MIX = 0.5

QUARTERS = 4
SCOPED = 32 * 1024 * 1024
HBM = pl.BlockSpec(memory_space=pltpu.HBM)
VMEM = pl.BlockSpec(memory_space=pltpu.VMEM)
PARAMS = pltpu.CompilerParams(vmem_limit_bytes=SCOPED)


def my_y(workers):
    return lax.axis_index("replica") // (workers // QUARTERS)


def place(y, k, width):
    quarter = jnp.bitwise_xor(y, k)
    per_fragment = QUARTERS // SYNCED
    return quarter // per_fragment, pl.ds(pl.multiple_of((quarter % per_fragment) * width, width), width)


def encode_kernel(workers, plan_hbm, local_hbm, outer_hbm, moment_hbm, *refs):
    out_refs, (outer_ref, local_ref, moment_ref, plan_ref, plan_sem, sems) = refs[:QUARTERS], refs[QUARTERS:]
    width = outer_ref.shape[-1]
    plan_copy = pltpu.make_async_copy(plan_hbm, plan_ref, plan_sem)
    plan_copy.start()
    y = my_y(workers)
    plan_copy.wait()
    order = (1, 2, 3, 0)
    copies = {}
    for k in order:
        number, cols = place(y, k, width)
        f = plan_ref[number]
        copies[k] = (
            pltpu.make_async_copy(outer_hbm.at[f, :, cols], outer_ref.at[k], sems.at[0, k]),
            pltpu.make_async_copy(local_hbm.at[0, f, :, cols], local_ref.at[k], sems.at[1, k]),
            pltpu.make_async_copy(moment_hbm.at[f, :, cols], moment_ref.at[k], sems.at[2, k]),
        )
        copies[k][0].start()
        copies[k][1].start()
    for k in order:
        copies[k][2].start()
    for k in order:
        copies[k][0].wait()
        copies[k][1].wait()
        for b in range(width // BLOCK):
            at = slice(b * BLOCK, (b + 1) * BLOCK)
            diff = outer_ref[k, :, at] - local_ref[k, :, at].astype(jnp.float32)
            scale = jnp.max(jnp.abs(diff), axis=-1, keepdims=True) + EPS
            out_refs[k][b] = (diff / scale).astype(jnp.bfloat16).astype(jnp.float32) * scale
    for k in order:
        copies[k][2].wait()


def encode(plan, local, outer, moment, workers):
    _, frags, rows, cols = local.shape
    width = SYNCED * cols // QUARTERS
    piece = jax.ShapeDtypeStruct((width // BLOCK, rows, BLOCK), jnp.float32)
    kept = lambda dtype: jax.ShapeDtypeStruct((QUARTERS, rows, width), dtype)
    return pl.pallas_call(
        lambda *refs: encode_kernel(workers, *refs),
        out_shape=(piece,) * QUARTERS + (kept(jnp.float32), kept(local.dtype), kept(jnp.float32)),
        in_specs=[HBM] * 4,
        out_specs=(VMEM,) * (QUARTERS + 3),
        scratch_shapes=[
            pltpu.SMEM(plan.shape, jnp.int32),
            pltpu.SemaphoreType.DMA(()),
            pltpu.SemaphoreType.DMA((3, QUARTERS)),
        ],
        compiler_params=PARAMS,
        name="encode",
    )(plan, local, outer, moment)


def add_kernel(*refs):
    *parts, out_ref = refs
    out_ref[...] = (parts[0][...] + parts[1][...]) + (parts[2][...] + parts[3][...])


def add(parts):
    return pl.pallas_call(
        add_kernel,
        out_shape=jax.ShapeDtypeStruct(parts[0].shape, jnp.float32),
        in_specs=[VMEM] * QUARTERS,
        out_specs=VMEM,
        compiler_params=PARAMS,
        name="add",
    )(*parts)


def mean_kernel(workers, parts_ref, out_ref):
    total = jnp.sum(parts_ref[...], axis=0) / workers
    out_ref[...] = jnp.broadcast_to(total[None], out_ref.shape)


def mean(parts, workers):
    return pl.pallas_call(
        lambda *refs: mean_kernel(workers, *refs),
        out_shape=jax.ShapeDtypeStruct(parts.shape, jnp.float32),
        in_specs=[VMEM],
        out_specs=VMEM,
        compiler_params=PARAMS,
        name="mean",
    )(parts)


def squares_kernel(workers, *refs):
    *quarters, out_ref = refs
    y = my_y(workers)
    row = lax.broadcasted_iota(jnp.int32, out_ref.shape, 0)
    total = jnp.zeros(out_ref.shape, jnp.float32)
    sums = [jnp.sum(q[...] * q[...]) for q in quarters]
    for k in range(0, QUARTERS, 2):
        number, _ = place(y, k, BLOCK)
        total = jnp.where(row == number, sums[k] + sums[k + 1], total)
    out_ref[...] = total


def squares(quarters, workers):
    return pl.pallas_call(
        lambda *refs: squares_kernel(workers, *refs),
        out_shape=jax.ShapeDtypeStruct((8, BLOCK), jnp.float32),
        in_specs=[VMEM] * QUARTERS,
        out_specs=VMEM,
        compiler_params=PARAMS,
        name="squares",
    )(*quarters)


def update_kernel(workers, entries, *refs):
    quarters, refs = refs[:QUARTERS], refs[QUARTERS:]
    squares_ref, outer_ref, local_ref, moment_ref, new_outer, new_moment, merged, outer_buf, moment_buf, merged_buf, factor_ref, sems = refs
    width = outer_ref.shape[-1]
    y = my_y(workers)
    factor_ref[...] = jnp.minimum(1.0, CLIP / jnp.sqrt(squares_ref[...] / entries + EPS))
    copies = []
    for k in range(QUARTERS):
        number, cols = place(y, k, width)
        factor = factor_ref[pl.ds(number, 1)]
        for b in range(width // BLOCK):
            at = slice(b * BLOCK, (b + 1) * BLOCK)
            grad = quarters[k][b] * factor
            moment_next = MU * moment_ref[k, :, at] + grad
            outer_next = outer_ref[k, :, at] - LR * (MU * moment_next + grad)
            moment_buf[k, :, at] = moment_next
            outer_buf[k, :, at] = outer_next
            merged_buf[k, :, at] = (
                MIX * local_ref[k, :, at].astype(jnp.float32) + (1.0 - MIX) * outer_next
            ).astype(jnp.bfloat16)
        copies += [
            pltpu.make_async_copy(moment_buf.at[k], new_moment.at[number, :, cols], sems.at[0, k]),
            pltpu.make_async_copy(outer_buf.at[k], new_outer.at[number, :, cols], sems.at[1, k]),
            pltpu.make_async_copy(merged_buf.at[k], merged.at[0, number, :, cols], sems.at[2, k]),
        ]
        for copy in copies[-3:]:
            copy.start()
    for copy in copies:
        copy.wait()


def update(quarters, squares_sum, outer_sel, local_sel, moment_sel, workers, entries):
    _, rows, width = outer_sel.shape
    cols = QUARTERS * width // SYNCED
    return pl.pallas_call(
        lambda *refs: update_kernel(workers, entries, *refs),
        out_shape=(
            jax.ShapeDtypeStruct((SYNCED, rows, cols), jnp.float32),
            jax.ShapeDtypeStruct((SYNCED, rows, cols), jnp.float32),
            jax.ShapeDtypeStruct((1, SYNCED, rows, cols), local_sel.dtype),
        ),
        in_specs=[VMEM] * (QUARTERS + 4),
        out_specs=(HBM,) * 3,
        scratch_shapes=[
            pltpu.VMEM(outer_sel.shape, jnp.float32),
            pltpu.VMEM(outer_sel.shape, jnp.float32),
            pltpu.VMEM(local_sel.shape, local_sel.dtype),
            pltpu.VMEM((8, BLOCK), jnp.float32),
            pltpu.SemaphoreType.DMA((3, QUARTERS)),
        ],
        compiler_params=PARAMS,
        name="update",
    )(*quarters, squares_sum, outer_sel, local_sel, moment_sel)


def shards(local, outer, moment, plan):
    _, frags, rows, cols = local.shape
    workers = lax.axis_size("replica")
    shares = lax.axis_size("mp")
    entries = rows * cols * shares
    inner = workers // QUARTERS
    groups = [list(range(g * inner, (g + 1) * inner)) for g in range(QUARTERS)]

    def along_y(array, k):
        return lax.ppermute(array, "replica", [(r, r ^ (k * inner)) for r in range(workers)])

    def inside(array):
        return lax.all_to_all(array, "replica", 0, 0, axis_index_groups=groups, tiled=True)

    *coded, outer_sel, local_sel, moment_sel = encode(plan, local, outer, moment, workers)
    mine = add([coded[0]] + [along_y(coded[k], k) for k in range(1, QUARTERS)])
    quarter = inside(mean(inside(mine), workers))
    quarters = [quarter] + [along_y(quarter, k) for k in range(1, QUARTERS)]
    squares_sum = squares(quarters, workers)
    for bit in (1, 2):
        squares_sum += lax.ppermute(squares_sum, "mp", [(m, m ^ bit) for m in range(shares)])
    return update(quarters, squares_sum, outer_sel, local_sel, moment_sel, workers, entries)


def solution(mesh):
    return jax.shard_map(
        shards,
        mesh=mesh,
        in_specs=(P("replica", None, None, "mp"), P(None, None, "mp"), P(None, None, "mp"), P()),
        out_specs=(P(None, None, "mp"), P(None, None, "mp"), P("replica", None, None, "mp")),
        check_vma=False,
    )
```

```python
import jax
import jax.numpy as jnp
from jax import lax
from jax.experimental import pallas as pl
from jax.experimental.pallas import tpu as pltpu
from jax.sharding import PartitionSpec as P

SYNCED = 2
BLOCK = 128
EPS = 1e-06
CLIP = 0.2
MU = 0.9
LR = 0.7
MIX = 0.5

QUARTERS = 4
SCOPED = 32 * 1024 * 1024
HBM = pl.BlockSpec(memory_space=pltpu.HBM)
VMEM = pl.BlockSpec(memory_space=pltpu.VMEM)
PARAMS = pltpu.CompilerParams(vmem_limit_bytes=SCOPED)


def my_y(workers):
    return lax.axis_index("replica") // (workers // QUARTERS)


def place(y, k, width):
    quarter = jnp.bitwise_xor(y, k)
    per_fragment = QUARTERS // SYNCED
    return quarter // per_fragment, pl.ds(pl.multiple_of((quarter % per_fragment) * width, width), width)


def encode_kernel(workers, plan_hbm, local_hbm, outer_hbm, moment_hbm, *refs):
    out_refs, (outer_ref, local_ref, moment_ref, plan_ref, plan_sem, sems) = refs[:QUARTERS], refs[QUARTERS:]
    width = outer_ref.shape[-1]
    plan_copy = pltpu.make_async_copy(plan_hbm, plan_ref, plan_sem)
    plan_copy.start()
    y = my_y(workers)
    plan_copy.wait()
    order = (1, 2, 3, 0)
    copies = {}
    for k in order:
        number, cols = place(y, k, width)
        f = plan_ref[number]
        copies[k] = (
            pltpu.make_async_copy(outer_hbm.at[f, :, cols], outer_ref.at[k], sems.at[0, k]),
            pltpu.make_async_copy(local_hbm.at[0, f, :, cols], local_ref.at[k], sems.at[1, k]),
            pltpu.make_async_copy(moment_hbm.at[f, :, cols], moment_ref.at[k], sems.at[2, k]),
        )
        copies[k][0].start()
        copies[k][1].start()
    for k in order:
        copies[k][2].start()
    for k in order:
        copies[k][0].wait()
        copies[k][1].wait()
        for b in range(width // BLOCK):
            at = slice(b * BLOCK, (b + 1) * BLOCK)
            diff = outer_ref[k, :, at] - local_ref[k, :, at].astype(jnp.float32)
            scale = jnp.max(jnp.abs(diff), axis=-1, keepdims=True) + EPS
            out_refs[k][b] = (diff / scale).astype(jnp.bfloat16).astype(jnp.float32) * scale
    for k in order:
        copies[k][2].wait()


def encode(plan, local, outer, moment, workers):
    _, frags, rows, cols = local.shape
    width = SYNCED * cols // QUARTERS
    piece = jax.ShapeDtypeStruct((width // BLOCK, rows, BLOCK), jnp.float32)
    kept = lambda dtype: jax.ShapeDtypeStruct((QUARTERS, rows, width), dtype)
    return pl.pallas_call(
        lambda *refs: encode_kernel(workers, *refs),
        out_shape=(piece,) * QUARTERS + (kept(jnp.float32), kept(local.dtype), kept(jnp.float32)),
        in_specs=[HBM] * 4,
        out_specs=(VMEM,) * (QUARTERS + 3),
        scratch_shapes=[
            pltpu.SMEM(plan.shape, jnp.int32),
            pltpu.SemaphoreType.DMA(()),
            pltpu.SemaphoreType.DMA((3, QUARTERS)),
        ],
        compiler_params=PARAMS,
        name="encode",
    )(*[pltpu.with_memory_space_constraint(a, pltpu.HBM) for a in (plan, local, outer, moment)])


def add_kernel(*refs):
    *parts, out_ref = refs
    out_ref[...] = (parts[0][...] + parts[1][...]) + (parts[2][...] + parts[3][...])


def add(parts):
    return pl.pallas_call(
        add_kernel,
        out_shape=jax.ShapeDtypeStruct(parts[0].shape, jnp.float32),
        in_specs=[VMEM] * QUARTERS,
        out_specs=VMEM,
        compiler_params=PARAMS,
        name="add",
    )(*parts)


def mean_kernel(workers, parts_ref, out_ref):
    total = jnp.sum(parts_ref[...], axis=0) / workers
    out_ref[...] = jnp.broadcast_to(total[None], out_ref.shape)


def mean(parts, workers):
    return pl.pallas_call(
        lambda *refs: mean_kernel(workers, *refs),
        out_shape=jax.ShapeDtypeStruct(parts.shape, jnp.float32),
        in_specs=[VMEM],
        out_specs=VMEM,
        compiler_params=PARAMS,
        name="mean",
    )(parts)


def squares_kernel(workers, *refs):
    *quarters, out_ref = refs
    y = my_y(workers)
    row = lax.broadcasted_iota(jnp.int32, out_ref.shape, 0)
    total = jnp.zeros(out_ref.shape, jnp.float32)
    sums = [jnp.sum(q[...] * q[...]) for q in quarters]
    for k in range(0, QUARTERS, 2):
        number, _ = place(y, k, BLOCK)
        total = jnp.where(row == number, sums[k] + sums[k + 1], total)
    out_ref[...] = total


def squares(quarters, workers):
    return pl.pallas_call(
        lambda *refs: squares_kernel(workers, *refs),
        out_shape=jax.ShapeDtypeStruct((8, BLOCK), jnp.float32),
        in_specs=[VMEM] * QUARTERS,
        out_specs=VMEM,
        compiler_params=PARAMS,
        name="squares",
    )(*quarters)


def update_kernel(workers, entries, *refs):
    quarters, refs = refs[:QUARTERS], refs[QUARTERS:]
    squares_ref, outer_ref, local_ref, moment_ref, new_outer, new_moment, merged, outer_buf, moment_buf, merged_buf, factor_ref, sems = refs
    width = outer_ref.shape[-1]
    y = my_y(workers)
    factor_ref[...] = jnp.minimum(1.0, CLIP / jnp.sqrt(squares_ref[...] / entries + EPS))
    copies = []
    for k in range(QUARTERS):
        number, cols = place(y, k, width)
        factor = factor_ref[pl.ds(number, 1)]
        for b in range(width // BLOCK):
            at = slice(b * BLOCK, (b + 1) * BLOCK)
            grad = quarters[k][b] * factor
            moment_next = MU * moment_ref[k, :, at] + grad
            outer_next = outer_ref[k, :, at] - LR * (MU * moment_next + grad)
            moment_buf[k, :, at] = moment_next
            outer_buf[k, :, at] = outer_next
            merged_buf[k, :, at] = (
                MIX * local_ref[k, :, at].astype(jnp.float32) + (1.0 - MIX) * outer_next
            ).astype(jnp.bfloat16)
        copies += [
            pltpu.make_async_copy(moment_buf.at[k], new_moment.at[number, :, cols], sems.at[0, k]),
            pltpu.make_async_copy(outer_buf.at[k], new_outer.at[number, :, cols], sems.at[1, k]),
            pltpu.make_async_copy(merged_buf.at[k], merged.at[0, number, :, cols], sems.at[2, k]),
        ]
        for copy in copies[-3:]:
            copy.start()
    for copy in copies:
        copy.wait()


def update(quarters, squares_sum, outer_sel, local_sel, moment_sel, workers, entries):
    _, rows, width = outer_sel.shape
    cols = QUARTERS * width // SYNCED
    return pl.pallas_call(
        lambda *refs: update_kernel(workers, entries, *refs),
        out_shape=(
            jax.ShapeDtypeStruct((SYNCED, rows, cols), jnp.float32),
            jax.ShapeDtypeStruct((SYNCED, rows, cols), jnp.float32),
            jax.ShapeDtypeStruct((1, SYNCED, rows, cols), local_sel.dtype),
        ),
        in_specs=[VMEM] * (QUARTERS + 4),
        out_specs=(HBM,) * 3,
        scratch_shapes=[
            pltpu.VMEM(outer_sel.shape, jnp.float32),
            pltpu.VMEM(outer_sel.shape, jnp.float32),
            pltpu.VMEM(local_sel.shape, local_sel.dtype),
            pltpu.VMEM((8, BLOCK), jnp.float32),
            pltpu.SemaphoreType.DMA((3, QUARTERS)),
        ],
        compiler_params=PARAMS,
        name="update",
    )(*quarters, squares_sum, outer_sel, local_sel, moment_sel)


def shards(local, outer, moment, plan):
    _, frags, rows, cols = local.shape
    workers = lax.axis_size("replica")
    shares = lax.axis_size("mp")
    entries = rows * cols * shares
    inner = workers // QUARTERS
    groups = [list(range(g * inner, (g + 1) * inner)) for g in range(QUARTERS)]

    def along_y(array, k):
        return lax.ppermute(array, "replica", [(r, r ^ (k * inner)) for r in range(workers)])

    def inside(array):
        return lax.all_to_all(array, "replica", 0, 0, axis_index_groups=groups, tiled=True)

    *coded, outer_sel, local_sel, moment_sel = encode(plan, local, outer, moment, workers)
    mine = add([coded[0]] + [along_y(coded[k], k) for k in range(1, QUARTERS)])
    quarter = inside(mean(inside(mine), workers))
    quarters = [quarter] + [along_y(quarter, k) for k in range(1, QUARTERS)]
    squares_sum = squares(quarters, workers)
    for bit in (1, 2):
        squares_sum += lax.ppermute(squares_sum, "mp", [(m, m ^ bit) for m in range(shares)])
    return update(quarters, squares_sum, outer_sel, local_sel, moment_sel, workers, entries)


def solution(mesh):
    return jax.shard_map(
        shards,
        mesh=mesh,
        in_specs=(P("replica", None, None, "mp"), P(None, None, "mp"), P(None, None, "mp"), P()),
        out_specs=(P(None, None, "mp"), P(None, None, "mp"), P("replica", None, None, "mp")),
        check_vma=False,
    )
```

```python
import jax
import jax.numpy as jnp
from jax import lax
from jax.experimental import pallas as pl
from jax.experimental.pallas import tpu as pltpu
from jax.sharding import PartitionSpec as P

SYNCED = 2
BLOCK = 128
EPS = 1e-06
CLIP = 0.2
MU = 0.9
LR = 0.7
MIX = 0.5

QUARTERS = 4
SCOPED = 32 * 1024 * 1024
HBM = pl.BlockSpec(memory_space=pltpu.HBM)
VMEM = pl.BlockSpec(memory_space=pltpu.VMEM)
PARAMS = pltpu.CompilerParams(vmem_limit_bytes=SCOPED)


SENT = (2, 3, 1)


def in_hbm(*arrays):
    return [pltpu.with_memory_space_constraint(array, pltpu.HBM) for array in arrays]


def my_y(workers):
    return lax.axis_index("replica") // (workers // QUARTERS)


def place(y, k, width):
    quarter = jnp.bitwise_xor(y, k)
    per_fragment = QUARTERS // SYNCED
    return quarter // per_fragment, pl.ds(pl.multiple_of((quarter % per_fragment) * width, width), width)


def coded(outer, local):
    diff = outer - local.astype(jnp.float32)
    scale = jnp.max(jnp.abs(diff), axis=-1, keepdims=True) + EPS
    return (diff / scale).astype(jnp.bfloat16).astype(jnp.float32) * scale


def encode_kernel(workers, plan_hbm, local_hbm, outer_hbm, *refs):
    out_refs, (outer_ref, local_ref, plan_ref, plan_sem, sems) = refs[: len(SENT)], refs[len(SENT) :]
    width = out_refs[0].shape[0] * BLOCK
    frags = outer_ref.shape[0]
    plan_copy = pltpu.make_async_copy(plan_hbm, plan_ref, plan_sem)
    plan_copy.start()
    copies = []
    for f in range(frags):
        copies.append(pltpu.make_async_copy(outer_hbm.at[f], outer_ref.at[f], sems.at[0, f]))
        copies.append(pltpu.make_async_copy(local_hbm.at[0, f], local_ref.at[f], sems.at[1, f]))
    for copy in copies:
        copy.start()
    y = my_y(workers)
    plan_copy.wait()
    for copy in copies:
        copy.wait()
    for k, out_ref in zip(SENT, out_refs):
        number, cols = place(y, k, width)
        f = plan_ref[number]
        for b in range(width // BLOCK):
            at = pl.ds(pl.multiple_of(cols.start + b * BLOCK, BLOCK), BLOCK)
            out_ref[b] = coded(outer_ref[f, :, at], local_ref[f, :, at])


def encode(plan, local, outer, workers):
    _, frags, rows, cols = local.shape
    width = SYNCED * cols // QUARTERS
    piece = jax.ShapeDtypeStruct((width // BLOCK, rows, BLOCK), jnp.float32)
    return pl.pallas_call(
        lambda *refs: encode_kernel(workers, *refs),
        out_shape=(piece,) * len(SENT),
        in_specs=[HBM] * 3,
        out_specs=(VMEM,) * len(SENT),
        scratch_shapes=[
            pltpu.VMEM(outer.shape, outer.dtype),
            pltpu.VMEM(local.shape[1:], local.dtype),
            pltpu.SMEM(plan.shape, jnp.int32),
            pltpu.SemaphoreType.DMA(()),
            pltpu.SemaphoreType.DMA((2, frags)),
        ],
        compiler_params=PARAMS,
        name="encode",
    )(*in_hbm(plan, local, outer))


def select_kernel(workers, plan_hbm, local_hbm, outer_hbm, moment_hbm, own_ref, outer_ref, local_ref, moment_ref, plan_ref, plan_sem, sems):
    width = outer_ref.shape[-1]
    plan_copy = pltpu.make_async_copy(plan_hbm, plan_ref, plan_sem)
    plan_copy.start()
    y = my_y(workers)
    plan_copy.wait()
    copies = []
    for k in range(QUARTERS):
        number, cols = place(y, k, width)
        f = plan_ref[number]
        copies += [
            pltpu.make_async_copy(outer_hbm.at[f, :, cols], outer_ref.at[k], sems.at[0, k]),
            pltpu.make_async_copy(local_hbm.at[0, f, :, cols], local_ref.at[k], sems.at[1, k]),
            pltpu.make_async_copy(moment_hbm.at[f, :, cols], moment_ref.at[k], sems.at[2, k]),
        ]
    for copy in copies:
        copy.start()
    for copy in copies:
        copy.wait()
    for b in range(width // BLOCK):
        at = slice(b * BLOCK, (b + 1) * BLOCK)
        own_ref[b] = coded(outer_ref[0, :, at], local_ref[0, :, at])


def select(plan, local, outer, moment, workers):
    _, frags, rows, cols = local.shape
    width = SYNCED * cols // QUARTERS
    kept = lambda dtype: jax.ShapeDtypeStruct((QUARTERS, rows, width), dtype)
    return pl.pallas_call(
        lambda *refs: select_kernel(workers, *refs),
        out_shape=(
            jax.ShapeDtypeStruct((width // BLOCK, rows, BLOCK), jnp.float32),
            kept(outer.dtype),
            kept(local.dtype),
            kept(moment.dtype),
        ),
        in_specs=[HBM] * 4,
        out_specs=(VMEM,) * 4,
        scratch_shapes=[
            pltpu.SMEM(plan.shape, jnp.int32),
            pltpu.SemaphoreType.DMA(()),
            pltpu.SemaphoreType.DMA((3, QUARTERS)),
        ],
        compiler_params=PARAMS,
        cost_estimate=pl.CostEstimate(flops=10**6, bytes_accessed=4 * 10**6, transcendentals=0),
        name="select",
    )(*in_hbm(plan, local, outer, moment))


def add_kernel(*refs):
    *parts, out_ref = refs
    out_ref[...] = (parts[0][...] + parts[1][...]) + (parts[2][...] + parts[3][...])


def add(parts):
    return pl.pallas_call(
        add_kernel,
        out_shape=jax.ShapeDtypeStruct(parts[0].shape, jnp.float32),
        in_specs=[VMEM] * QUARTERS,
        out_specs=VMEM,
        compiler_params=PARAMS,
        name="add",
    )(*parts)


def mean_kernel(workers, parts_ref, out_ref):
    total = jnp.sum(parts_ref[...], axis=0) / workers
    out_ref[...] = jnp.broadcast_to(total[None], out_ref.shape)


def mean(parts, workers):
    return pl.pallas_call(
        lambda *refs: mean_kernel(workers, *refs),
        out_shape=jax.ShapeDtypeStruct(parts.shape, jnp.float32),
        in_specs=[VMEM],
        out_specs=VMEM,
        compiler_params=PARAMS,
        name="mean",
    )(parts)


def squares_kernel(workers, *refs):
    *quarters, out_ref = refs
    y = my_y(workers)
    row = lax.broadcasted_iota(jnp.int32, out_ref.shape, 0)
    total = jnp.zeros(out_ref.shape, jnp.float32)
    sums = [jnp.sum(q[...] * q[...]) for q in quarters]
    for k in range(0, QUARTERS, 2):
        number, _ = place(y, k, BLOCK)
        total = jnp.where(row == number, sums[k] + sums[k + 1], total)
    out_ref[...] = total


def squares(quarters, workers):
    return pl.pallas_call(
        lambda *refs: squares_kernel(workers, *refs),
        out_shape=jax.ShapeDtypeStruct((8, BLOCK), jnp.float32),
        in_specs=[VMEM] * QUARTERS,
        out_specs=VMEM,
        compiler_params=PARAMS,
        name="squares",
    )(*quarters)


def update_kernel(workers, entries, *refs):
    quarters, refs = refs[:QUARTERS], refs[QUARTERS:]
    squares_ref, outer_ref, local_ref, moment_ref, new_outer, new_moment, merged, outer_buf, moment_buf, merged_buf, factor_ref, sems = refs
    width = outer_ref.shape[-1]
    y = my_y(workers)
    factor_ref[...] = jnp.minimum(1.0, CLIP / jnp.sqrt(squares_ref[...] / entries + EPS))
    copies = []
    for k in range(QUARTERS):
        number, cols = place(y, k, width)
        factor = factor_ref[pl.ds(number, 1)]
        for b in range(width // BLOCK):
            at = slice(b * BLOCK, (b + 1) * BLOCK)
            grad = quarters[k][b] * factor
            moment_next = MU * moment_ref[k, :, at] + grad
            outer_next = outer_ref[k, :, at] - LR * (MU * moment_next + grad)
            moment_buf[k, :, at] = moment_next
            outer_buf[k, :, at] = outer_next
            merged_buf[k, :, at] = (
                MIX * local_ref[k, :, at].astype(jnp.float32) + (1.0 - MIX) * outer_next
            ).astype(jnp.bfloat16)
        copies += [
            pltpu.make_async_copy(moment_buf.at[k], new_moment.at[number, :, cols], sems.at[0, k]),
            pltpu.make_async_copy(outer_buf.at[k], new_outer.at[number, :, cols], sems.at[1, k]),
            pltpu.make_async_copy(merged_buf.at[k], merged.at[0, number, :, cols], sems.at[2, k]),
        ]
        for copy in copies[-3:]:
            copy.start()
    for copy in copies:
        copy.wait()


def update(quarters, squares_sum, outer_sel, local_sel, moment_sel, workers, entries):
    _, rows, width = outer_sel.shape
    cols = QUARTERS * width // SYNCED
    return pl.pallas_call(
        lambda *refs: update_kernel(workers, entries, *refs),
        out_shape=(
            jax.ShapeDtypeStruct((SYNCED, rows, cols), jnp.float32),
            jax.ShapeDtypeStruct((SYNCED, rows, cols), jnp.float32),
            jax.ShapeDtypeStruct((1, SYNCED, rows, cols), local_sel.dtype),
        ),
        in_specs=[VMEM] * (QUARTERS + 4),
        out_specs=(HBM,) * 3,
        scratch_shapes=[
            pltpu.VMEM(outer_sel.shape, jnp.float32),
            pltpu.VMEM(outer_sel.shape, jnp.float32),
            pltpu.VMEM(local_sel.shape, local_sel.dtype),
            pltpu.VMEM((8, BLOCK), jnp.float32),
            pltpu.SemaphoreType.DMA((3, QUARTERS)),
        ],
        compiler_params=PARAMS,
        name="update",
    )(*quarters, squares_sum, outer_sel, local_sel, moment_sel)


def shards(local, outer, moment, plan):
    _, frags, rows, cols = local.shape
    workers = lax.axis_size("replica")
    shares = lax.axis_size("mp")
    entries = rows * cols * shares
    inner = workers // QUARTERS
    groups = [list(range(g * inner, (g + 1) * inner)) for g in range(QUARTERS)]

    def along_y(array, k):
        return lax.ppermute(array, "replica", [(r, r ^ (k * inner)) for r in range(workers)])

    def inside(array):
        return lax.all_to_all(array, "replica", 0, 0, axis_index_groups=groups, tiled=True)

    sent = encode(plan, local, outer, workers)
    arrived = [along_y(array, k) for k, array in zip(SENT, sent)]
    own, outer_sel, local_sel, moment_sel = select(plan, local, outer, moment, workers)
    mine = add([own] + arrived)
    quarter = inside(mean(inside(mine), workers))
    received = {k: along_y(quarter, k) for k in reversed(SENT)}
    quarters = [quarter] + [received[k] for k in range(1, QUARTERS)]
    squares_sum = squares(quarters, workers)
    for bit in (1, 2):
        squares_sum += lax.ppermute(squares_sum, "mp", [(m, m ^ bit) for m in range(shares)])
    return update(quarters, squares_sum, outer_sel, local_sel, moment_sel, workers, entries)


def solution(mesh):
    return jax.shard_map(
        shards,
        mesh=mesh,
        in_specs=(P("replica", None, None, "mp"), P(None, None, "mp"), P(None, None, "mp"), P()),
        out_specs=(P(None, None, "mp"), P(None, None, "mp"), P("replica", None, None, "mp")),
        check_vma=False,
    )
```

```python
import jax
import jax.numpy as jnp
from jax import lax
from jax.experimental import pallas as pl
from jax.experimental.pallas import tpu as pltpu
from jax.sharding import PartitionSpec as P

SYNCED = 2
BLOCK = 128
EPS = 1e-06
CLIP = 0.2
MU = 0.9
LR = 0.7
MIX = 0.5

QUARTERS = 4
SCOPED = 32 * 1024 * 1024
HBM = pl.BlockSpec(memory_space=pltpu.HBM)
VMEM = pl.BlockSpec(memory_space=pltpu.VMEM)
PARAMS = pltpu.CompilerParams(vmem_limit_bytes=SCOPED)


SENT = (2, 3, 1)
HELD = (0, 1, 3, 2)


def in_hbm(*arrays):
    return [pltpu.with_memory_space_constraint(array, pltpu.HBM) for array in arrays]


def my_y(workers):
    return lax.axis_index("replica") // (workers // QUARTERS)


def place(y, k, width):
    quarter = jnp.bitwise_xor(y, k)
    per_fragment = QUARTERS // SYNCED
    return quarter // per_fragment, pl.ds(pl.multiple_of((quarter % per_fragment) * width, width), width)


def coded(outer, local):
    diff = outer - local.astype(jnp.float32)
    scale = jnp.max(jnp.abs(diff), axis=-1, keepdims=True) + EPS
    return (diff / scale).astype(jnp.bfloat16).astype(jnp.float32) * scale


def encode_kernel(workers, plan_hbm, local_hbm, outer_hbm, *refs):
    out_refs, (outer_ref, local_ref, plan_ref, plan_sem, sems) = refs[: len(SENT)], refs[len(SENT) :]
    width = out_refs[0].shape[0] * BLOCK
    frags = outer_ref.shape[0]
    plan_copy = pltpu.make_async_copy(plan_hbm, plan_ref, plan_sem)
    plan_copy.start()
    def copies(f):
        return (
            pltpu.make_async_copy(outer_hbm.at[f], outer_ref.at[f], sems.at[0, f]),
            pltpu.make_async_copy(local_hbm.at[0, f], local_ref.at[f], sems.at[1, f]),
        )

    for f in range(frags):
        for copy in copies(f):
            copy.start()
    y = my_y(workers)
    plan_copy.wait()
    waited = set()
    for k, out_ref in zip(SENT, out_refs):
        number, cols = place(y, k, width)
        f = plan_ref[number]
        if k // 2 not in waited:
            waited.add(k // 2)
            for copy in copies(f):
                copy.wait()
        for b in range(width // BLOCK):
            at = pl.ds(pl.multiple_of(cols.start + b * BLOCK, BLOCK), BLOCK)
            out_ref[b] = coded(outer_ref[f, :, at], local_ref[f, :, at])
    for number in range(SYNCED, frags):
        for copy in copies(plan_ref[number]):
            copy.wait()


def encode(plan, local, outer, workers):
    _, frags, rows, cols = local.shape
    width = SYNCED * cols // QUARTERS
    piece = jax.ShapeDtypeStruct((width // BLOCK, rows, BLOCK), jnp.float32)
    return pl.pallas_call(
        lambda *refs: encode_kernel(workers, *refs),
        out_shape=(piece,) * len(SENT),
        in_specs=[HBM] * 3,
        out_specs=(VMEM,) * len(SENT),
        scratch_shapes=[
            pltpu.VMEM(outer.shape, outer.dtype),
            pltpu.VMEM(local.shape[1:], local.dtype),
            pltpu.SMEM(plan.shape, jnp.int32),
            pltpu.SemaphoreType.DMA(()),
            pltpu.SemaphoreType.DMA((2, frags)),
        ],
        compiler_params=PARAMS,
        name="encode",
    )(*in_hbm(plan, local, outer))


def select_kernel(workers, plan_hbm, local_hbm, outer_hbm, moment_hbm, own_ref, outer_ref, local_ref, moment_ref, plan_ref, plan_sem, sems):
    width = outer_ref.shape[-1]
    plan_copy = pltpu.make_async_copy(plan_hbm, plan_ref, plan_sem)
    plan_copy.start()
    y = my_y(workers)
    plan_copy.wait()
    copies = []
    for k in range(QUARTERS):
        number, cols = place(y, k, width)
        f = plan_ref[number]
        copies += [
            pltpu.make_async_copy(outer_hbm.at[f, :, cols], outer_ref.at[k], sems.at[0, k]),
            pltpu.make_async_copy(local_hbm.at[0, f, :, cols], local_ref.at[k], sems.at[1, k]),
            pltpu.make_async_copy(moment_hbm.at[f, :, cols], moment_ref.at[k], sems.at[2, k]),
        ]
    for copy in copies:
        copy.start()
    for copy in copies:
        copy.wait()
    for b in range(width // BLOCK):
        at = slice(b * BLOCK, (b + 1) * BLOCK)
        own_ref[b] = coded(outer_ref[0, :, at], local_ref[0, :, at])


def select(plan, local, outer, moment, workers):
    _, frags, rows, cols = local.shape
    width = SYNCED * cols // QUARTERS
    kept = lambda dtype: jax.ShapeDtypeStruct((QUARTERS, rows, width), dtype)
    return pl.pallas_call(
        lambda *refs: select_kernel(workers, *refs),
        out_shape=(
            jax.ShapeDtypeStruct((width // BLOCK, rows, BLOCK), jnp.float32),
            kept(outer.dtype),
            kept(local.dtype),
            kept(moment.dtype),
        ),
        in_specs=[HBM] * 4,
        out_specs=(VMEM,) * 4,
        scratch_shapes=[
            pltpu.SMEM(plan.shape, jnp.int32),
            pltpu.SemaphoreType.DMA(()),
            pltpu.SemaphoreType.DMA((3, QUARTERS)),
        ],
        compiler_params=PARAMS,
        cost_estimate=pl.CostEstimate(flops=10**6, bytes_accessed=4 * 10**6, transcendentals=0),
        name="select",
    )(*in_hbm(plan, local, outer, moment))


def add_kernel(*refs):
    *parts, out_ref = refs
    out_ref[...] = (parts[0][...] + parts[1][...]) + (parts[2][...] + parts[3][...])


def add(parts):
    return pl.pallas_call(
        add_kernel,
        out_shape=jax.ShapeDtypeStruct(parts[0].shape, jnp.float32),
        in_specs=[VMEM] * QUARTERS,
        out_specs=VMEM,
        compiler_params=PARAMS,
        name="add",
    )(*parts)


def mean_kernel(workers, parts_ref, out_ref):
    total = jnp.sum(parts_ref[...], axis=0) / workers
    out_ref[...] = jnp.broadcast_to(total[None], out_ref.shape)


def mean(parts, workers):
    return pl.pallas_call(
        lambda *refs: mean_kernel(workers, *refs),
        out_shape=jax.ShapeDtypeStruct(parts.shape, jnp.float32),
        in_specs=[VMEM],
        out_specs=VMEM,
        compiler_params=PARAMS,
        name="mean",
    )(parts)


def squares_kernel(workers, *refs):
    *quarters, out_ref = refs
    y = my_y(workers)
    row = lax.broadcasted_iota(jnp.int32, out_ref.shape, 0)
    total = jnp.zeros(out_ref.shape, jnp.float32)
    sums = {k: jnp.sum(q[...] * q[...]) for k, q in zip(HELD, quarters)}
    for k in range(0, QUARTERS, 2):
        number, _ = place(y, k, BLOCK)
        total = jnp.where(row == number, sums[k] + sums[k + 1], total)
    out_ref[...] = total


def squares(quarters, workers):
    return pl.pallas_call(
        lambda *refs: squares_kernel(workers, *refs),
        out_shape=jax.ShapeDtypeStruct((8, BLOCK), jnp.float32),
        in_specs=[VMEM] * QUARTERS,
        out_specs=VMEM,
        compiler_params=PARAMS,
        name="squares",
    )(*quarters)


def update_kernel(workers, entries, *refs):
    quarters, refs = refs[:QUARTERS], refs[QUARTERS:]
    early_ref, back_ref, outer_ref, local_ref, moment_ref, new_outer, new_moment, merged, outer_buf, moment_buf, merged_buf, factor_ref, sems = refs
    width = outer_ref.shape[-1]
    y = my_y(workers)
    total = jnp.where(lax.axis_index("mp") % 2 == 1, early_ref[...], back_ref[...])
    factor_ref[...] = jnp.minimum(1.0, CLIP / jnp.sqrt(total / entries + EPS))
    copies = []
    for quarter_ref, k in zip(quarters, HELD):
        number, cols = place(y, k, width)
        factor = factor_ref[pl.ds(number, 1)]
        for b in range(width // BLOCK):
            at = slice(b * BLOCK, (b + 1) * BLOCK)
            grad = quarter_ref[b] * factor
            moment_next = MU * moment_ref[k, :, at] + grad
            outer_next = outer_ref[k, :, at] - LR * (MU * moment_next + grad)
            moment_buf[k, :, at] = moment_next
            outer_buf[k, :, at] = outer_next
            merged_buf[k, :, at] = (
                MIX * local_ref[k, :, at].astype(jnp.float32) + (1.0 - MIX) * outer_next
            ).astype(jnp.bfloat16)
        copies += [
            pltpu.make_async_copy(moment_buf.at[k], new_moment.at[number, :, cols], sems.at[0, k]),
            pltpu.make_async_copy(outer_buf.at[k], new_outer.at[number, :, cols], sems.at[1, k]),
            pltpu.make_async_copy(merged_buf.at[k], merged.at[0, number, :, cols], sems.at[2, k]),
        ]
        for copy in copies[-3:]:
            copy.start()
    for copy in copies:
        copy.wait()


def update(quarters, totals, outer_sel, local_sel, moment_sel, workers, entries):
    _, rows, width = outer_sel.shape
    cols = QUARTERS * width // SYNCED
    return pl.pallas_call(
        lambda *refs: update_kernel(workers, entries, *refs),
        out_shape=(
            jax.ShapeDtypeStruct((SYNCED, rows, cols), jnp.float32),
            jax.ShapeDtypeStruct((SYNCED, rows, cols), jnp.float32),
            jax.ShapeDtypeStruct((1, SYNCED, rows, cols), local_sel.dtype),
        ),
        in_specs=[VMEM] * (QUARTERS + 5),
        out_specs=(HBM,) * 3,
        scratch_shapes=[
            pltpu.VMEM(outer_sel.shape, jnp.float32),
            pltpu.VMEM(outer_sel.shape, jnp.float32),
            pltpu.VMEM(local_sel.shape, local_sel.dtype),
            pltpu.VMEM((8, BLOCK), jnp.float32),
            pltpu.SemaphoreType.DMA((3, QUARTERS)),
        ],
        compiler_params=PARAMS,
        name="update",
    )(*quarters, *totals, outer_sel, local_sel, moment_sel)


def shards(local, outer, moment, plan):
    _, frags, rows, cols = local.shape
    workers = lax.axis_size("replica")
    shares = lax.axis_size("mp")
    entries = rows * cols * shares
    inner = workers // QUARTERS
    groups = [list(range(g * inner, (g + 1) * inner)) for g in range(QUARTERS)]

    def along_y(array, k):
        return lax.ppermute(array, "replica", [(r, r ^ (k * inner)) for r in range(workers)])

    def inside(array):
        return lax.all_to_all(array, "replica", 0, 0, axis_index_groups=groups, tiled=True)

    sent = encode(plan, local, outer, workers)
    arrived = [along_y(array, k) for k, array in zip(SENT, sent)]
    own, outer_sel, local_sel, moment_sel = select(plan, local, outer, moment, workers)
    mine = add([own] + arrived)
    quarter = inside(mean(inside(mine), workers))
    received = {k: along_y(quarter, k) for k in SENT}
    quarters = [quarter] + [received[k] for k in HELD[1:]]
    return update(quarters, mp_totals(squares(quarters, workers)), outer_sel, local_sel, moment_sel, workers, entries)


def mp_totals(mine):
    from_late = [lax.ppermute(mine, "mp", pairs) for pairs in ([(0, 3), (2, 1)], [(0, 1), (2, 3)])]
    from_early = lax.ppermute(mine, "mp", [(1, 3), (3, 1)])
    total = (mine + from_early) + (from_late[0] + from_late[1])
    return total, lax.ppermute(total, "mp", [(1, 0), (3, 2)])


def solution(mesh):
    return jax.shard_map(
        shards,
        mesh=mesh,
        in_specs=(P("replica", None, None, "mp"), P(None, None, "mp"), P(None, None, "mp"), P()),
        out_specs=(P(None, None, "mp"), P(None, None, "mp"), P("replica", None, None, "mp")),
        check_vma=False,
    )
```

```python
import jax
import jax.numpy as jnp
from jax import lax
from jax.experimental import pallas as pl
from jax.experimental.pallas import tpu as pltpu
from jax.sharding import PartitionSpec as P

SYNCED = 2
BLOCK = 128
EPS = 1e-06
CLIP = 0.2
MU = 0.9
LR = 0.7
MIX = 0.5

QUARTERS = 4
SCOPED = 32 * 1024 * 1024
HBM = pl.BlockSpec(memory_space=pltpu.HBM)
VMEM = pl.BlockSpec(memory_space=pltpu.VMEM)
PARAMS = pltpu.CompilerParams(vmem_limit_bytes=SCOPED)


SENT = (2, 3, 1)
HELD = (0, 1, 3, 2)


def in_hbm(*arrays):
    return [pltpu.with_memory_space_constraint(array, pltpu.HBM) for array in arrays]


def my_y(workers):
    return lax.axis_index("replica") // (workers // QUARTERS)


def place(y, k, width):
    quarter = jnp.bitwise_xor(y, k)
    per_fragment = QUARTERS // SYNCED
    return quarter // per_fragment, pl.ds(pl.multiple_of((quarter % per_fragment) * width, width), width)


def coded(outer, local):
    diff = outer - local.astype(jnp.float32)
    scale = jnp.max(jnp.abs(diff), axis=-1, keepdims=True) + EPS
    return (diff / scale).astype(jnp.bfloat16).astype(jnp.float32) * scale


def encode_kernel(workers, plan_hbm, local_hbm, outer_hbm, *refs):
    out_refs, (outer_ref, local_ref, plan_ref, plan_sem, sems) = refs[: len(SENT)], refs[len(SENT) :]
    width = out_refs[0].shape[0] * BLOCK
    frags = outer_ref.shape[0]
    plan_copy = pltpu.make_async_copy(plan_hbm, plan_ref, plan_sem)
    plan_copy.start()
    def copies(f):
        return (
            pltpu.make_async_copy(outer_hbm.at[f], outer_ref.at[f], sems.at[0, f]),
            pltpu.make_async_copy(local_hbm.at[0, f], local_ref.at[f], sems.at[1, f]),
        )

    for f in range(frags):
        for copy in copies(f):
            copy.start()
    y = my_y(workers)
    plan_copy.wait()
    waited = set()
    for k, out_ref in zip(SENT, out_refs):
        number, cols = place(y, k, width)
        f = plan_ref[number]
        if k // 2 not in waited:
            waited.add(k // 2)
            for copy in copies(f):
                copy.wait()
        for b in range(width // BLOCK):
            at = pl.ds(pl.multiple_of(cols.start + b * BLOCK, BLOCK), BLOCK)
            out_ref[b] = coded(outer_ref[f, :, at], local_ref[f, :, at])
    for number in range(SYNCED, frags):
        for copy in copies(plan_ref[number]):
            copy.wait()


def encode(plan, local, outer, workers):
    _, frags, rows, cols = local.shape
    width = SYNCED * cols // QUARTERS
    piece = jax.ShapeDtypeStruct((width // BLOCK, rows, BLOCK), jnp.float32)
    return pl.pallas_call(
        lambda *refs: encode_kernel(workers, *refs),
        out_shape=(piece,) * len(SENT),
        in_specs=[HBM] * 3,
        out_specs=(VMEM,) * len(SENT),
        scratch_shapes=[
            pltpu.VMEM(outer.shape, outer.dtype),
            pltpu.VMEM(local.shape[1:], local.dtype),
            pltpu.SMEM(plan.shape, jnp.int32),
            pltpu.SemaphoreType.DMA(()),
            pltpu.SemaphoreType.DMA((2, frags)),
        ],
        compiler_params=PARAMS,
        name="encode",
    )(*in_hbm(plan, local, outer))


def select_kernel(workers, plan_hbm, local_hbm, outer_hbm, moment_hbm, own_ref, outer_ref, local_ref, moment_ref, plan_ref, plan_sem, sems):
    width = outer_ref.shape[-1]
    plan_copy = pltpu.make_async_copy(plan_hbm, plan_ref, plan_sem)
    plan_copy.start()
    y = my_y(workers)
    plan_copy.wait()
    copies = []
    for k in range(QUARTERS):
        number, cols = place(y, k, width)
        f = plan_ref[number]
        copies += [
            pltpu.make_async_copy(outer_hbm.at[f, :, cols], outer_ref.at[k], sems.at[0, k]),
            pltpu.make_async_copy(local_hbm.at[0, f, :, cols], local_ref.at[k], sems.at[1, k]),
            pltpu.make_async_copy(moment_hbm.at[f, :, cols], moment_ref.at[k], sems.at[2, k]),
        ]
    for copy in copies:
        copy.start()
    for copy in copies:
        copy.wait()
    for b in range(width // BLOCK):
        at = slice(b * BLOCK, (b + 1) * BLOCK)
        own_ref[b] = coded(outer_ref[0, :, at], local_ref[0, :, at])


def select(plan, local, outer, moment, workers):
    _, frags, rows, cols = local.shape
    width = SYNCED * cols // QUARTERS
    kept = lambda dtype: jax.ShapeDtypeStruct((QUARTERS, rows, width), dtype)
    return pl.pallas_call(
        lambda *refs: select_kernel(workers, *refs),
        out_shape=(
            jax.ShapeDtypeStruct((width // BLOCK, rows, BLOCK), jnp.float32),
            kept(outer.dtype),
            kept(local.dtype),
            kept(moment.dtype),
        ),
        in_specs=[HBM] * 4,
        out_specs=(VMEM,) * 4,
        scratch_shapes=[
            pltpu.SMEM(plan.shape, jnp.int32),
            pltpu.SemaphoreType.DMA(()),
            pltpu.SemaphoreType.DMA((3, QUARTERS)),
        ],
        compiler_params=PARAMS,
        cost_estimate=pl.CostEstimate(flops=10**6, bytes_accessed=4 * 10**6, transcendentals=0),
        name="select",
    )(*in_hbm(plan, local, outer, moment))


def add_kernel(*refs):
    *parts, out_ref = refs
    out_ref[...] = (parts[0][...] + parts[1][...]) + (parts[2][...] + parts[3][...])


def add(parts):
    return pl.pallas_call(
        add_kernel,
        out_shape=jax.ShapeDtypeStruct(parts[0].shape, jnp.float32),
        in_specs=[VMEM] * QUARTERS,
        out_specs=VMEM,
        compiler_params=PARAMS,
        name="add",
    )(*parts)


def mean_kernel(workers, parts_ref, out_ref):
    total = jnp.sum(parts_ref[...], axis=0) / workers
    out_ref[...] = jnp.broadcast_to(total[None], out_ref.shape)


def mean(parts, workers):
    return pl.pallas_call(
        lambda *refs: mean_kernel(workers, *refs),
        out_shape=jax.ShapeDtypeStruct(parts.shape, jnp.float32),
        in_specs=[VMEM],
        out_specs=VMEM,
        compiler_params=PARAMS,
        name="mean",
    )(parts)


def squares_kernel(workers, *refs):
    *quarters, out_ref = refs
    y = my_y(workers)
    row = lax.broadcasted_iota(jnp.int32, out_ref.shape, 0)
    total = jnp.zeros(out_ref.shape, jnp.float32)
    sums = {k: jnp.sum(q[...] * q[...]) for k, q in zip(HELD, quarters)}
    for k in range(0, QUARTERS, 2):
        number, _ = place(y, k, BLOCK)
        total = jnp.where(row == number, sums[k] + sums[k + 1], total)
    out_ref[...] = total


def squares(quarters, workers):
    return pl.pallas_call(
        lambda *refs: squares_kernel(workers, *refs),
        out_shape=jax.ShapeDtypeStruct((8, BLOCK), jnp.float32),
        in_specs=[VMEM] * QUARTERS,
        out_specs=VMEM,
        compiler_params=PARAMS,
        name="squares",
    )(*quarters)


def update_kernel(workers, entries, *refs):
    quarters, refs = refs[:QUARTERS], refs[QUARTERS:]
    squares_ref, outer_ref, local_ref, moment_ref, new_outer, new_moment, merged, outer_buf, moment_buf, merged_buf, factor_ref, sems = refs
    width = outer_ref.shape[-1]
    y = my_y(workers)
    factor_ref[...] = jnp.minimum(1.0, CLIP / jnp.sqrt(squares_ref[...] / entries + EPS))
    copies = []
    for quarter_ref, k in zip(quarters, HELD):
        number, cols = place(y, k, width)
        factor = factor_ref[pl.ds(number, 1)]
        for b in range(width // BLOCK):
            at = slice(b * BLOCK, (b + 1) * BLOCK)
            grad = quarter_ref[b] * factor
            moment_next = MU * moment_ref[k, :, at] + grad
            outer_next = outer_ref[k, :, at] - LR * (MU * moment_next + grad)
            moment_buf[k, :, at] = moment_next
            outer_buf[k, :, at] = outer_next
            merged_buf[k, :, at] = (
                MIX * local_ref[k, :, at].astype(jnp.float32) + (1.0 - MIX) * outer_next
            ).astype(jnp.bfloat16)
        copies += [
            pltpu.make_async_copy(moment_buf.at[k], new_moment.at[number, :, cols], sems.at[0, k]),
            pltpu.make_async_copy(outer_buf.at[k], new_outer.at[number, :, cols], sems.at[1, k]),
            pltpu.make_async_copy(merged_buf.at[k], merged.at[0, number, :, cols], sems.at[2, k]),
        ]
        for copy in copies[-3:]:
            copy.start()
    for copy in copies:
        copy.wait()


def update(quarters, squares_sum, outer_sel, local_sel, moment_sel, workers, entries):
    _, rows, width = outer_sel.shape
    cols = QUARTERS * width // SYNCED
    return pl.pallas_call(
        lambda *refs: update_kernel(workers, entries, *refs),
        out_shape=(
            jax.ShapeDtypeStruct((SYNCED, rows, cols), jnp.float32),
            jax.ShapeDtypeStruct((SYNCED, rows, cols), jnp.float32),
            jax.ShapeDtypeStruct((1, SYNCED, rows, cols), local_sel.dtype),
        ),
        in_specs=[VMEM] * (QUARTERS + 4),
        out_specs=(HBM,) * 3,
        scratch_shapes=[
            pltpu.VMEM(outer_sel.shape, jnp.float32),
            pltpu.VMEM(outer_sel.shape, jnp.float32),
            pltpu.VMEM(local_sel.shape, local_sel.dtype),
            pltpu.VMEM((8, BLOCK), jnp.float32),
            pltpu.SemaphoreType.DMA((3, QUARTERS)),
        ],
        compiler_params=PARAMS,
        name="update",
    )(*quarters, squares_sum, outer_sel, local_sel, moment_sel)


def shards(local, outer, moment, plan):
    _, frags, rows, cols = local.shape
    workers = lax.axis_size("replica")
    shares = lax.axis_size("mp")
    entries = rows * cols * shares
    inner = workers // QUARTERS
    groups = [list(range(g * inner, (g + 1) * inner)) for g in range(QUARTERS)]

    def along_y(array, k):
        return lax.ppermute(array, "replica", [(r, r ^ (k * inner)) for r in range(workers)])

    def inside(array):
        return lax.all_to_all(array, "replica", 0, 0, axis_index_groups=groups, tiled=True)

    sent = encode(plan, local, outer, workers)
    arrived = [along_y(array, k) for k, array in zip(SENT, sent)]
    own, outer_sel, local_sel, moment_sel = select(plan, local, outer, moment, workers)
    mine = add([own] + arrived)
    quarter = inside(mean(inside(mine), workers))
    received = {k: along_y(quarter, k) for k in SENT}
    quarters = [quarter] + [received[k] for k in HELD[1:]]
    return update(quarters, mp_total(squares(quarters, workers)), outer_sel, local_sel, moment_sel, workers, entries)


def mp_total(mine):
    swap = {bit: lax.ppermute(mine, "mp", [(m, m ^ bit) for m in range(4)]) for bit in (2, 3, 1)}
    return (mine + swap[1]) + (swap[3] + swap[2])


def solution(mesh):
    return jax.shard_map(
        shards,
        mesh=mesh,
        in_specs=(P("replica", None, None, "mp"), P(None, None, "mp"), P(None, None, "mp"), P()),
        out_specs=(P(None, None, "mp"), P(None, None, "mp"), P("replica", None, None, "mp")),
        check_vma=False,
    )
```

```python
import jax
import jax.numpy as jnp
from jax import lax
from jax.experimental import pallas as pl
from jax.experimental.pallas import tpu as pltpu
from jax.sharding import PartitionSpec as P

SYNCED = 2
BLOCK = 128
TILE = 8
EPS = 1e-06
CLIP = 0.2
MU = 0.9
LR = 0.7
MIX = 0.5

QUARTERS = 4
SCOPED = 32 * 1024 * 1024
HBM = pl.BlockSpec(memory_space=pltpu.HBM)
VMEM = pl.BlockSpec(memory_space=pltpu.VMEM)
PARAMS = pltpu.CompilerParams(vmem_limit_bytes=SCOPED)


SENT = (2, 3, 1)


def in_hbm(*arrays):
    return [pltpu.with_memory_space_constraint(array, pltpu.HBM) for array in arrays]


def my_y(workers):
    return lax.axis_index("replica") // (workers // QUARTERS)


def place(y, k, width):
    quarter = jnp.bitwise_xor(y, k)
    per_fragment = QUARTERS // SYNCED
    return quarter // per_fragment, pl.ds(pl.multiple_of((quarter % per_fragment) * width, width), width)


def coded(outer, local):
    diff = outer - local.astype(jnp.float32)
    scale = jnp.max(jnp.abs(diff), axis=-1, keepdims=True) + EPS
    return (diff / scale).astype(jnp.bfloat16).astype(jnp.float32) * scale


def encode_kernel(workers, plan_hbm, local_hbm, outer_hbm, *refs):
    out_refs, (outer_ref, local_ref, plan_ref, plan_sem, sems) = refs[: len(SENT)], refs[len(SENT) :]
    width = out_refs[0].shape[0] * BLOCK
    frags = outer_ref.shape[0]
    plan_copy = pltpu.make_async_copy(plan_hbm, plan_ref, plan_sem)
    plan_copy.start()
    def copies(f):
        return (
            pltpu.make_async_copy(outer_hbm.at[f], outer_ref.at[f], sems.at[0, f]),
            pltpu.make_async_copy(local_hbm.at[0, f], local_ref.at[f], sems.at[1, f]),
        )

    for f in range(frags):
        for copy in copies(f):
            copy.start()
    y = my_y(workers)
    plan_copy.wait()
    waited = set()
    for k, out_ref in zip(SENT, out_refs):
        number, cols = place(y, k, width)
        f = plan_ref[number]
        if k // 2 not in waited:
            waited.add(k // 2)
            for copy in copies(f):
                copy.wait()
        for b in range(width // BLOCK):
            at = pl.ds(pl.multiple_of(cols.start + b * BLOCK, BLOCK), BLOCK)
            out_ref[b] = coded(outer_ref[f, :, at], local_ref[f, :, at])
    for number in range(SYNCED, frags):
        for copy in copies(plan_ref[number]):
            copy.wait()


def encode(plan, local, outer, workers):
    _, frags, rows, cols = local.shape
    width = SYNCED * cols // QUARTERS
    piece = jax.ShapeDtypeStruct((width // BLOCK, rows, BLOCK), jnp.float32)
    return pl.pallas_call(
        lambda *refs: encode_kernel(workers, *refs),
        out_shape=(piece,) * len(SENT),
        in_specs=[HBM] * 3,
        out_specs=(VMEM,) * len(SENT),
        scratch_shapes=[
            pltpu.VMEM(outer.shape, outer.dtype),
            pltpu.VMEM(local.shape[1:], local.dtype),
            pltpu.SMEM(plan.shape, jnp.int32),
            pltpu.SemaphoreType.DMA(()),
            pltpu.SemaphoreType.DMA((2, frags)),
        ],
        compiler_params=PARAMS,
        name="encode",
    )(*in_hbm(plan, local, outer))


def select_kernel(workers, plan_hbm, local_hbm, outer_hbm, moment_hbm, own_ref, outer_ref, local_ref, moment_ref, plan_ref, plan_sem, sems):
    width = outer_ref.shape[-1]
    plan_copy = pltpu.make_async_copy(plan_hbm, plan_ref, plan_sem)
    plan_copy.start()
    y = my_y(workers)
    plan_copy.wait()
    copies = []
    for k in range(QUARTERS):
        number, cols = place(y, k, width)
        f = plan_ref[number]
        copies += [
            pltpu.make_async_copy(outer_hbm.at[f, :, cols], outer_ref.at[k], sems.at[0, k]),
            pltpu.make_async_copy(local_hbm.at[0, f, :, cols], local_ref.at[k], sems.at[1, k]),
            pltpu.make_async_copy(moment_hbm.at[f, :, cols], moment_ref.at[k], sems.at[2, k]),
        ]
    for copy in copies:
        copy.start()
    for copy in copies:
        copy.wait()
    for b in range(width // BLOCK):
        at = slice(b * BLOCK, (b + 1) * BLOCK)
        own_ref[b] = coded(outer_ref[0, :, at], local_ref[0, :, at])


def select(plan, local, outer, moment, workers):
    _, frags, rows, cols = local.shape
    width = SYNCED * cols // QUARTERS
    kept = lambda dtype: jax.ShapeDtypeStruct((QUARTERS, rows, width), dtype)
    return pl.pallas_call(
        lambda *refs: select_kernel(workers, *refs),
        out_shape=(
            jax.ShapeDtypeStruct((width // BLOCK, rows, BLOCK), jnp.float32),
            kept(outer.dtype),
            kept(local.dtype),
            kept(moment.dtype),
        ),
        in_specs=[HBM] * 4,
        out_specs=(VMEM,) * 4,
        scratch_shapes=[
            pltpu.SMEM(plan.shape, jnp.int32),
            pltpu.SemaphoreType.DMA(()),
            pltpu.SemaphoreType.DMA((3, QUARTERS)),
        ],
        compiler_params=PARAMS,
        cost_estimate=pl.CostEstimate(flops=10**6, bytes_accessed=4 * 10**6, transcendentals=0),
        name="select",
    )(*in_hbm(plan, local, outer, moment))


def add_kernel(*refs):
    *parts, out_ref = refs
    out_ref[...] = (parts[0][...] + parts[1][...]) + (parts[2][...] + parts[3][...])


def add(parts):
    return pl.pallas_call(
        add_kernel,
        out_shape=jax.ShapeDtypeStruct(parts[0].shape, jnp.float32),
        in_specs=[VMEM] * QUARTERS,
        out_specs=VMEM,
        compiler_params=PARAMS,
        name="add",
    )(*parts)


def mean_kernel(workers, parts_ref, out_ref):
    total = jnp.sum(parts_ref[...], axis=0) / workers
    out_ref[...] = jnp.broadcast_to(total[None], out_ref.shape)


def mean(parts, workers):
    return pl.pallas_call(
        lambda *refs: mean_kernel(workers, *refs),
        out_shape=jax.ShapeDtypeStruct(parts.shape, jnp.float32),
        in_specs=[VMEM],
        out_specs=VMEM,
        compiler_params=PARAMS,
        name="mean",
    )(parts)


def squares_kernel(quarter_ref, out_ref, held_ref):
    quarter = quarter_ref[...]
    out_ref[...] = jnp.broadcast_to(jnp.sum(quarter * quarter), out_ref.shape)
    held_ref[...] = quarter


def squares(quarter):
    return pl.pallas_call(
        squares_kernel,
        out_shape=(
            jax.ShapeDtypeStruct((TILE, BLOCK), jnp.float32),
            jax.ShapeDtypeStruct(quarter.shape, jnp.float32),
        ),
        in_specs=[VMEM],
        out_specs=(VMEM, VMEM),
        compiler_params=PARAMS,
        name="squares",
    )(quarter)


def pack_kernel(core_ref, cross_ref, side_ref, early_ref, mine_ref, quarter_ref, out_ref, total_ref):
    pieces, rows, _ = quarter_ref.shape
    total = (mine_ref[...] + core_ref[...]) + (cross_ref[...] + side_ref[...])
    total_ref[...] = total
    out_ref[pieces * rows :] = total
    for b in range(pieces):
        out_ref[b * rows : (b + 1) * rows] = quarter_ref[b]


def pack(swaps, early, mine, quarter):
    pieces, rows, _ = quarter.shape
    operands = (*swaps, early, mine, quarter)
    return pl.pallas_call(
        pack_kernel,
        out_shape=(
            jax.ShapeDtypeStruct((pieces * rows + TILE, BLOCK), jnp.float32),
            jax.ShapeDtypeStruct(mine.shape, jnp.float32),
        ),
        in_specs=[VMEM] * len(operands),
        out_specs=(VMEM, VMEM),
        compiler_params=PARAMS,
        name="pack",
    )(*operands)


def update_kernel(workers, entries, own_ref, own_total_ref, far_ref, far_total_ref, third_ref, near_ref, outer_ref, local_ref, moment_ref, new_outer, new_moment, merged, outer_buf, moment_buf, merged_buf, sems):
    pieces, rows, _ = own_ref.shape
    width = outer_ref.shape[-1]
    y = my_y(workers)
    tail = slice(pieces * rows, pieces * rows + TILE)

    def factor_of(total):
        factor = jnp.minimum(1.0, CLIP / jnp.sqrt(total / entries + EPS))
        return jnp.concatenate([factor] * (rows // TILE), axis=0)

    near = factor_of(own_total_ref[...] + near_ref[tail])
    far = factor_of(far_total_ref[...] + third_ref[tail])
    packed = lambda ref: lambda b: ref[b * rows : (b + 1) * rows]
    pieces_of = lambda ref: lambda b: ref[b]
    copies = []
    for k, piece, factor in (
        (0, pieces_of(own_ref), near),
        (2, pieces_of(far_ref), far),
        (3, packed(third_ref), far),
        (1, packed(near_ref), near),
    ):
        number, cols = place(y, k, width)
        for b in range(pieces):
            at = slice(b * BLOCK, (b + 1) * BLOCK)
            grad = piece(b) * factor
            moment_next = MU * moment_ref[k, :, at] + grad
            outer_next = outer_ref[k, :, at] - LR * (MU * moment_next + grad)
            moment_buf[k, :, at] = moment_next
            outer_buf[k, :, at] = outer_next
            merged_buf[k, :, at] = (
                MIX * local_ref[k, :, at].astype(jnp.float32) + (1.0 - MIX) * outer_next
            ).astype(jnp.bfloat16)
        copies += [
            pltpu.make_async_copy(moment_buf.at[k], new_moment.at[number, :, cols], sems.at[0, k]),
            pltpu.make_async_copy(outer_buf.at[k], new_outer.at[number, :, cols], sems.at[1, k]),
            pltpu.make_async_copy(merged_buf.at[k], merged.at[0, number, :, cols], sems.at[2, k]),
        ]
        for copy in copies[-3:]:
            copy.start()
    for copy in copies:
        copy.wait()


def update(means, outer_sel, local_sel, moment_sel, workers, entries):
    _, rows, width = outer_sel.shape
    cols = QUARTERS * width // SYNCED
    return pl.pallas_call(
        lambda *refs: update_kernel(workers, entries, *refs),
        out_shape=(
            jax.ShapeDtypeStruct((SYNCED, rows, cols), jnp.float32),
            jax.ShapeDtypeStruct((SYNCED, rows, cols), jnp.float32),
            jax.ShapeDtypeStruct((1, SYNCED, rows, cols), local_sel.dtype),
        ),
        in_specs=[VMEM] * (len(means) + 3),
        out_specs=(HBM,) * 3,
        scratch_shapes=[
            pltpu.VMEM(outer_sel.shape, jnp.float32),
            pltpu.VMEM(outer_sel.shape, jnp.float32),
            pltpu.VMEM(local_sel.shape, local_sel.dtype),
            pltpu.SemaphoreType.DMA((3, QUARTERS)),
        ],
        compiler_params=PARAMS,
        name="update",
    )(*means, outer_sel, local_sel, moment_sel)


def shards(local, outer, moment, plan):
    _, frags, rows, cols = local.shape
    workers = lax.axis_size("replica")
    shares = lax.axis_size("mp")
    entries = rows * cols * shares
    inner = workers // QUARTERS
    groups = [list(range(g * inner, (g + 1) * inner)) for g in range(QUARTERS)]

    def along_y(array, k):
        return lax.ppermute(array, "replica", [(r, r ^ (k * inner)) for r in range(workers)])

    def inside(array):
        return lax.all_to_all(array, "replica", 0, 0, axis_index_groups=groups, tiled=True)

    sent = encode(plan, local, outer, workers)
    arrived = [along_y(array, k) for k, array in zip(SENT, sent)]
    own, outer_sel, local_sel, moment_sel = select(plan, local, outer, moment, workers)
    mine = add([own] + arrived)
    raw = inside(mean(inside(mine), workers))
    own_squares, quarter = squares(raw)
    far = along_y(raw, 2)
    swaps = [lax.ppermute(own_squares, "mp", [(m, m ^ bit) for m in range(shares)]) for bit in (1, 3, 2)]
    packed, total = pack(swaps, far, own_squares, quarter)
    third, near, far_total = along_y(packed, 3), along_y(packed, 1), along_y(total, 2)
    return update((quarter, total, far, far_total, third, near), outer_sel, local_sel, moment_sel, workers, entries)


def solution(mesh):
    return jax.shard_map(
        shards,
        mesh=mesh,
        in_specs=(P("replica", None, None, "mp"), P(None, None, "mp"), P(None, None, "mp"), P()),
        out_specs=(P(None, None, "mp"), P(None, None, "mp"), P("replica", None, None, "mp")),
        check_vma=False,
    )
```

```python
import jax
import jax.numpy as jnp
from jax import lax
from jax.experimental import pallas as pl
from jax.experimental.pallas import tpu as pltpu
from jax.sharding import PartitionSpec as P

SYNCED = 2
BLOCK = 128
TILE = 8
EPS = 1e-06
CLIP = 0.2
MU = 0.9
LR = 0.7
MIX = 0.5

QUARTERS = 4
SCOPED = 32 * 1024 * 1024
HBM = pl.BlockSpec(memory_space=pltpu.HBM)
VMEM = pl.BlockSpec(memory_space=pltpu.VMEM)
PARAMS = pltpu.CompilerParams(vmem_limit_bytes=SCOPED)


SENT = (2, 3, 1)


def in_hbm(*arrays):
    return [pltpu.with_memory_space_constraint(array, pltpu.HBM) for array in arrays]


def my_y(workers):
    return lax.axis_index("replica") // (workers // QUARTERS)


def place(y, k, width):
    quarter = jnp.bitwise_xor(y, k)
    per_fragment = QUARTERS // SYNCED
    return quarter // per_fragment, pl.ds(pl.multiple_of((quarter % per_fragment) * width, width), width)


def coded(outer, local):
    diff = outer - local.astype(jnp.float32)
    scale = jnp.max(jnp.abs(diff), axis=-1, keepdims=True) + EPS
    return (diff / scale).astype(jnp.bfloat16).astype(jnp.float32) * scale


def encode_kernel(workers, plan_hbm, local_hbm, outer_hbm, *refs):
    out_refs, (outer_ref, local_ref, plan_ref, plan_sem, sems) = refs[: len(SENT)], refs[len(SENT) :]
    width = out_refs[0].shape[0] * BLOCK
    frags = outer_ref.shape[0]
    plan_copy = pltpu.make_async_copy(plan_hbm, plan_ref, plan_sem)
    plan_copy.start()
    def copies(f):
        return (
            pltpu.make_async_copy(outer_hbm.at[f], outer_ref.at[f], sems.at[0, f]),
            pltpu.make_async_copy(local_hbm.at[0, f], local_ref.at[f], sems.at[1, f]),
        )

    for f in range(frags):
        for copy in copies(f):
            copy.start()
    y = my_y(workers)
    plan_copy.wait()
    waited = set()
    for k, out_ref in zip(SENT, out_refs):
        number, cols = place(y, k, width)
        f = plan_ref[number]
        if k // 2 not in waited:
            waited.add(k // 2)
            for copy in copies(f):
                copy.wait()
        for b in range(width // BLOCK):
            at = pl.ds(pl.multiple_of(cols.start + b * BLOCK, BLOCK), BLOCK)
            out_ref[b] = coded(outer_ref[f, :, at], local_ref[f, :, at])
    for number in range(SYNCED, frags):
        for copy in copies(plan_ref[number]):
            copy.wait()


def encode(plan, local, outer, workers):
    _, frags, rows, cols = local.shape
    width = SYNCED * cols // QUARTERS
    piece = jax.ShapeDtypeStruct((width // BLOCK, rows, BLOCK), jnp.float32)
    return pl.pallas_call(
        lambda *refs: encode_kernel(workers, *refs),
        out_shape=(piece,) * len(SENT),
        in_specs=[HBM] * 3,
        out_specs=(VMEM,) * len(SENT),
        scratch_shapes=[
            pltpu.VMEM(outer.shape, outer.dtype),
            pltpu.VMEM(local.shape[1:], local.dtype),
            pltpu.SMEM(plan.shape, jnp.int32),
            pltpu.SemaphoreType.DMA(()),
            pltpu.SemaphoreType.DMA((2, frags)),
        ],
        compiler_params=PARAMS,
        name="encode",
    )(*in_hbm(plan, local, outer))


def select_kernel(workers, plan_hbm, local_hbm, outer_hbm, moment_hbm, own_ref, outer_ref, local_ref, moment_ref, plan_ref, plan_sem, sems):
    width = outer_ref.shape[-1]
    plan_copy = pltpu.make_async_copy(plan_hbm, plan_ref, plan_sem)
    plan_copy.start()
    y = my_y(workers)
    plan_copy.wait()
    copies = []
    for k in range(QUARTERS):
        number, cols = place(y, k, width)
        f = plan_ref[number]
        copies += [
            pltpu.make_async_copy(outer_hbm.at[f, :, cols], outer_ref.at[k], sems.at[0, k]),
            pltpu.make_async_copy(local_hbm.at[0, f, :, cols], local_ref.at[k], sems.at[1, k]),
            pltpu.make_async_copy(moment_hbm.at[f, :, cols], moment_ref.at[k], sems.at[2, k]),
        ]
    for copy in copies:
        copy.start()
    for copy in copies:
        copy.wait()
    for b in range(width // BLOCK):
        at = slice(b * BLOCK, (b + 1) * BLOCK)
        own_ref[b] = coded(outer_ref[0, :, at], local_ref[0, :, at])


def select(plan, local, outer, moment, workers):
    _, frags, rows, cols = local.shape
    width = SYNCED * cols // QUARTERS
    kept = lambda dtype: jax.ShapeDtypeStruct((QUARTERS, rows, width), dtype)
    return pl.pallas_call(
        lambda *refs: select_kernel(workers, *refs),
        out_shape=(
            jax.ShapeDtypeStruct((width // BLOCK, rows, BLOCK), jnp.float32),
            kept(outer.dtype),
            kept(local.dtype),
            kept(moment.dtype),
        ),
        in_specs=[HBM] * 4,
        out_specs=(VMEM,) * 4,
        scratch_shapes=[
            pltpu.SMEM(plan.shape, jnp.int32),
            pltpu.SemaphoreType.DMA(()),
            pltpu.SemaphoreType.DMA((3, QUARTERS)),
        ],
        compiler_params=PARAMS,
        cost_estimate=pl.CostEstimate(flops=10**6, bytes_accessed=4 * 10**6, transcendentals=0),
        name="select",
    )(*in_hbm(plan, local, outer, moment))


def add_kernel(*refs):
    *parts, out_ref = refs
    out_ref[...] = (parts[0][...] + parts[1][...]) + (parts[2][...] + parts[3][...])


def add(parts):
    return pl.pallas_call(
        add_kernel,
        out_shape=jax.ShapeDtypeStruct(parts[0].shape, jnp.float32),
        in_specs=[VMEM] * QUARTERS,
        out_specs=VMEM,
        compiler_params=PARAMS,
        name="add",
    )(*parts)


def mean_kernel(workers, parts_ref, out_ref):
    total = jnp.sum(parts_ref[...], axis=0) / workers
    out_ref[...] = jnp.broadcast_to(total[None], out_ref.shape)


def mean(parts, workers):
    return pl.pallas_call(
        lambda *refs: mean_kernel(workers, *refs),
        out_shape=jax.ShapeDtypeStruct(parts.shape, jnp.float32),
        in_specs=[VMEM],
        out_specs=VMEM,
        compiler_params=PARAMS,
        name="mean",
    )(parts)


def squares_kernel(quarter_ref, out_ref, held_ref):
    quarter = quarter_ref[...]
    out_ref[...] = jnp.broadcast_to(jnp.sum(quarter * quarter), out_ref.shape)
    held_ref[...] = quarter


def squares(quarter):
    return pl.pallas_call(
        squares_kernel,
        out_shape=(
            jax.ShapeDtypeStruct((TILE, BLOCK), jnp.float32),
            jax.ShapeDtypeStruct(quarter.shape, jnp.float32),
        ),
        in_specs=[VMEM],
        out_specs=(VMEM, VMEM),
        compiler_params=PARAMS,
        name="squares",
    )(quarter)


def pack_kernel(core_ref, cross_ref, side_ref, early_ref, mine_ref, quarter_ref, out_ref, total_ref):
    pieces, rows, _ = quarter_ref.shape
    total = (mine_ref[...] + core_ref[...]) + (cross_ref[...] + side_ref[...])
    total_ref[...] = total
    out_ref[pieces * rows :] = total
    for b in range(pieces):
        out_ref[b * rows : (b + 1) * rows] = quarter_ref[b]


def pack(swaps, early, mine, quarter):
    pieces, rows, _ = quarter.shape
    operands = (*swaps, early, mine, quarter)
    return pl.pallas_call(
        pack_kernel,
        out_shape=(
            jax.ShapeDtypeStruct((pieces * rows + TILE, BLOCK), jnp.float32),
            jax.ShapeDtypeStruct(mine.shape, jnp.float32),
        ),
        in_specs=[VMEM] * len(operands),
        out_specs=(VMEM, VMEM),
        compiler_params=PARAMS,
        name="pack",
    )(*operands)


def update_kernel(workers, entries, own_ref, own_total_ref, far_ref, near_ref, third_ref, far_total_ref, outer_ref, local_ref, moment_ref, new_outer, new_moment, merged, outer_buf, moment_buf, merged_buf, sems):
    pieces, rows, _ = own_ref.shape
    width = outer_ref.shape[-1]
    y = my_y(workers)
    tail = slice(pieces * rows, pieces * rows + TILE)

    def factor_of(total):
        factor = jnp.minimum(1.0, CLIP / jnp.sqrt(total / entries + EPS))
        return jnp.concatenate([factor] * (rows // TILE), axis=0)

    near = factor_of(own_total_ref[...] + near_ref[tail])
    far = factor_of(far_total_ref[...] + third_ref[tail])
    packed = lambda ref: lambda b: ref[b * rows : (b + 1) * rows]
    pieces_of = lambda ref: lambda b: ref[b]
    copies = []
    for k, piece, factor in (
        (0, pieces_of(own_ref), near),
        (2, pieces_of(far_ref), far),
        (3, packed(third_ref), far),
        (1, packed(near_ref), near),
    ):
        number, cols = place(y, k, width)
        for b in range(pieces):
            at = slice(b * BLOCK, (b + 1) * BLOCK)
            grad = piece(b) * factor
            moment_next = MU * moment_ref[k, :, at] + grad
            outer_next = outer_ref[k, :, at] - LR * (MU * moment_next + grad)
            moment_buf[k, :, at] = moment_next
            outer_buf[k, :, at] = outer_next
            merged_buf[k, :, at] = (
                MIX * local_ref[k, :, at].astype(jnp.float32) + (1.0 - MIX) * outer_next
            ).astype(jnp.bfloat16)
        copies += [
            pltpu.make_async_copy(moment_buf.at[k], new_moment.at[number, :, cols], sems.at[0, k]),
            pltpu.make_async_copy(outer_buf.at[k], new_outer.at[number, :, cols], sems.at[1, k]),
            pltpu.make_async_copy(merged_buf.at[k], merged.at[0, number, :, cols], sems.at[2, k]),
        ]
        for copy in copies[-3:]:
            copy.start()
    for copy in copies:
        copy.wait()


def update(means, outer_sel, local_sel, moment_sel, workers, entries):
    _, rows, width = outer_sel.shape
    cols = QUARTERS * width // SYNCED
    return pl.pallas_call(
        lambda *refs: update_kernel(workers, entries, *refs),
        out_shape=(
            jax.ShapeDtypeStruct((SYNCED, rows, cols), jnp.float32),
            jax.ShapeDtypeStruct((SYNCED, rows, cols), jnp.float32),
            jax.ShapeDtypeStruct((1, SYNCED, rows, cols), local_sel.dtype),
        ),
        in_specs=[VMEM] * (len(means) + 3),
        out_specs=(HBM,) * 3,
        scratch_shapes=[
            pltpu.VMEM(outer_sel.shape, jnp.float32),
            pltpu.VMEM(outer_sel.shape, jnp.float32),
            pltpu.VMEM(local_sel.shape, local_sel.dtype),
            pltpu.SemaphoreType.DMA((3, QUARTERS)),
        ],
        compiler_params=PARAMS,
        name="update",
    )(*means, outer_sel, local_sel, moment_sel)


def shards(local, outer, moment, plan):
    _, frags, rows, cols = local.shape
    workers = lax.axis_size("replica")
    shares = lax.axis_size("mp")
    entries = rows * cols * shares
    inner = workers // QUARTERS
    groups = [list(range(g * inner, (g + 1) * inner)) for g in range(QUARTERS)]

    def along_y(array, k):
        return lax.ppermute(array, "replica", [(r, r ^ (k * inner)) for r in range(workers)])

    def inside(array):
        return lax.all_to_all(array, "replica", 0, 0, axis_index_groups=groups, tiled=True)

    sent = encode(plan, local, outer, workers)
    arrived = [along_y(array, k) for k, array in zip(SENT, sent)]
    own, outer_sel, local_sel, moment_sel = select(plan, local, outer, moment, workers)
    mine = add([own] + arrived)
    raw = inside(mean(inside(mine), workers))
    own_squares, quarter = squares(raw)
    far = along_y(raw, 2)
    swaps = [lax.ppermute(own_squares, "mp", [(m, m ^ bit) for m in range(shares)]) for bit in (1, 3, 2)]
    packed, total = pack(swaps, far, own_squares, quarter)
    near, third, far_total = along_y(packed, 1), along_y(packed, 3), along_y(total, 2)
    return update((quarter, total, far, near, third, far_total), outer_sel, local_sel, moment_sel, workers, entries)


def solution(mesh):
    return jax.shard_map(
        shards,
        mesh=mesh,
        in_specs=(P("replica", None, None, "mp"), P(None, None, "mp"), P(None, None, "mp"), P()),
        out_specs=(P(None, None, "mp"), P(None, None, "mp"), P("replica", None, None, "mp")),
        check_vma=False,
    )
```

```python
import jax
import jax.numpy as jnp
from jax import lax
from jax.experimental import pallas as pl
from jax.experimental.pallas import tpu as pltpu
from jax.sharding import PartitionSpec as P

SYNCED = 2
BLOCK = 128
TILE = 8
EPS = 1e-06
CLIP = 0.2
MU = 0.9
LR = 0.7
MIX = 0.5

QUARTERS = 4
SCOPED = 32 * 1024 * 1024
HBM = pl.BlockSpec(memory_space=pltpu.HBM)
VMEM = pl.BlockSpec(memory_space=pltpu.VMEM)
PARAMS = pltpu.CompilerParams(vmem_limit_bytes=SCOPED)


SENT = (2, 3, 1)


def in_hbm(*arrays):
    return [pltpu.with_memory_space_constraint(array, pltpu.HBM) for array in arrays]


def my_y(workers):
    return lax.axis_index("replica") // (workers // QUARTERS)


def place(y, k, width):
    quarter = jnp.bitwise_xor(y, k)
    per_fragment = QUARTERS // SYNCED
    return quarter // per_fragment, pl.ds(pl.multiple_of((quarter % per_fragment) * width, width), width)


def coded(outer, local):
    diff = outer - local.astype(jnp.float32)
    scale = jnp.max(jnp.abs(diff), axis=-1, keepdims=True) + EPS
    return (diff / scale).astype(jnp.bfloat16).astype(jnp.float32) * scale


def encode_kernel(workers, plan_hbm, local_hbm, outer_hbm, *refs):
    out_refs, (outer_ref, local_ref, plan_ref, plan_sem, sems) = refs[: len(SENT)], refs[len(SENT) :]
    width = out_refs[0].shape[0] * BLOCK
    frags = outer_ref.shape[0]
    plan_copy = pltpu.make_async_copy(plan_hbm, plan_ref, plan_sem)
    plan_copy.start()
    def copies(f):
        return (
            pltpu.make_async_copy(outer_hbm.at[f], outer_ref.at[f], sems.at[0, f]),
            pltpu.make_async_copy(local_hbm.at[0, f], local_ref.at[f], sems.at[1, f]),
        )

    for f in range(frags):
        for copy in copies(f):
            copy.start()
    y = my_y(workers)
    plan_copy.wait()
    for f in range(frags):
        for copy in copies(f):
            copy.wait()
    for k, out_ref in zip(SENT, out_refs):
        number, cols = place(y, k, width)
        f = plan_ref[number]
        for b in range(width // BLOCK):
            at = pl.ds(pl.multiple_of(cols.start + b * BLOCK, BLOCK), BLOCK)
            out_ref[b] = coded(outer_ref[f, :, at], local_ref[f, :, at])


def encode(plan, local, outer, workers):
    _, frags, rows, cols = local.shape
    width = SYNCED * cols // QUARTERS
    piece = jax.ShapeDtypeStruct((width // BLOCK, rows, BLOCK), jnp.float32)
    return pl.pallas_call(
        lambda *refs: encode_kernel(workers, *refs),
        out_shape=(piece,) * len(SENT),
        in_specs=[HBM] * 3,
        out_specs=(VMEM,) * len(SENT),
        scratch_shapes=[
            pltpu.VMEM(outer.shape, outer.dtype),
            pltpu.VMEM(local.shape[1:], local.dtype),
            pltpu.SMEM(plan.shape, jnp.int32),
            pltpu.SemaphoreType.DMA(()),
            pltpu.SemaphoreType.DMA((2, frags)),
        ],
        compiler_params=PARAMS,
        name="encode",
    )(*in_hbm(plan, local, outer))


def select_kernel(workers, plan_hbm, local_hbm, outer_hbm, moment_hbm, own_ref, outer_ref, local_ref, moment_ref, plan_ref, plan_sem, sems):
    width = outer_ref.shape[-1]
    plan_copy = pltpu.make_async_copy(plan_hbm, plan_ref, plan_sem)
    plan_copy.start()
    y = my_y(workers)
    plan_copy.wait()
    copies = []
    for k in range(QUARTERS):
        number, cols = place(y, k, width)
        f = plan_ref[number]
        copies += [
            pltpu.make_async_copy(outer_hbm.at[f, :, cols], outer_ref.at[k], sems.at[0, k]),
            pltpu.make_async_copy(local_hbm.at[0, f, :, cols], local_ref.at[k], sems.at[1, k]),
            pltpu.make_async_copy(moment_hbm.at[f, :, cols], moment_ref.at[k], sems.at[2, k]),
        ]
    for copy in copies:
        copy.start()
    for copy in copies:
        copy.wait()
    for b in range(width // BLOCK):
        at = slice(b * BLOCK, (b + 1) * BLOCK)
        own_ref[b] = coded(outer_ref[0, :, at], local_ref[0, :, at])


def select(plan, local, outer, moment, workers):
    _, frags, rows, cols = local.shape
    width = SYNCED * cols // QUARTERS
    kept = lambda dtype: jax.ShapeDtypeStruct((QUARTERS, rows, width), dtype)
    return pl.pallas_call(
        lambda *refs: select_kernel(workers, *refs),
        out_shape=(
            jax.ShapeDtypeStruct((width // BLOCK, rows, BLOCK), jnp.float32),
            kept(outer.dtype),
            kept(local.dtype),
            kept(moment.dtype),
        ),
        in_specs=[HBM] * 4,
        out_specs=(VMEM,) * 4,
        scratch_shapes=[
            pltpu.SMEM(plan.shape, jnp.int32),
            pltpu.SemaphoreType.DMA(()),
            pltpu.SemaphoreType.DMA((3, QUARTERS)),
        ],
        compiler_params=PARAMS,
        cost_estimate=pl.CostEstimate(flops=10**6, bytes_accessed=4 * 10**6, transcendentals=0),
        name="select",
    )(*in_hbm(plan, local, outer, moment))


def add_kernel(*refs):
    *parts, out_ref = refs
    out_ref[...] = (parts[0][...] + parts[1][...]) + (parts[2][...] + parts[3][...])


def add(parts):
    return pl.pallas_call(
        add_kernel,
        out_shape=jax.ShapeDtypeStruct(parts[0].shape, jnp.float32),
        in_specs=[VMEM] * QUARTERS,
        out_specs=VMEM,
        compiler_params=PARAMS,
        name="add",
    )(*parts)


def mean_kernel(workers, parts_ref, out_ref):
    total = jnp.sum(parts_ref[...], axis=0) / workers
    out_ref[...] = jnp.broadcast_to(total[None], out_ref.shape)


def mean(parts, workers):
    return pl.pallas_call(
        lambda *refs: mean_kernel(workers, *refs),
        out_shape=jax.ShapeDtypeStruct(parts.shape, jnp.float32),
        in_specs=[VMEM],
        out_specs=VMEM,
        compiler_params=PARAMS,
        name="mean",
    )(parts)


def squares_kernel(quarter_ref, out_ref, held_ref):
    quarter = quarter_ref[...]
    out_ref[...] = jnp.broadcast_to(jnp.sum(quarter * quarter), out_ref.shape)
    held_ref[...] = quarter


def squares(quarter):
    return pl.pallas_call(
        squares_kernel,
        out_shape=(
            jax.ShapeDtypeStruct((TILE, BLOCK), jnp.float32),
            jax.ShapeDtypeStruct(quarter.shape, jnp.float32),
        ),
        in_specs=[VMEM],
        out_specs=(VMEM, VMEM),
        compiler_params=PARAMS,
        name="squares",
    )(quarter)


def pack_kernel(core_ref, cross_ref, side_ref, early_ref, mine_ref, quarter_ref, out_ref, total_ref):
    pieces, rows, _ = quarter_ref.shape
    total = (mine_ref[...] + core_ref[...]) + (cross_ref[...] + side_ref[...])
    total_ref[...] = total
    out_ref[pieces * rows :] = total
    for b in range(pieces):
        out_ref[b * rows : (b + 1) * rows] = quarter_ref[b]


def pack(swaps, early, mine, quarter):
    pieces, rows, _ = quarter.shape
    operands = (*swaps, early, mine, quarter)
    return pl.pallas_call(
        pack_kernel,
        out_shape=(
            jax.ShapeDtypeStruct((pieces * rows + TILE, BLOCK), jnp.float32),
            jax.ShapeDtypeStruct(mine.shape, jnp.float32),
        ),
        in_specs=[VMEM] * len(operands),
        out_specs=(VMEM, VMEM),
        compiler_params=PARAMS,
        name="pack",
    )(*operands)


def update_kernel(workers, entries, own_ref, own_total_ref, far_ref, far_total_ref, third_ref, near_ref, outer_ref, local_ref, moment_ref, new_outer, new_moment, merged, outer_buf, moment_buf, merged_buf, sems):
    pieces, rows, _ = own_ref.shape
    width = outer_ref.shape[-1]
    y = my_y(workers)
    tail = slice(pieces * rows, pieces * rows + TILE)

    def factor_of(total):
        factor = jnp.minimum(1.0, CLIP / jnp.sqrt(total / entries + EPS))
        return jnp.concatenate([factor] * (rows // TILE), axis=0)

    near = factor_of(own_total_ref[...] + near_ref[tail])
    far = factor_of(far_total_ref[...] + third_ref[tail])
    packed = lambda ref: lambda b: ref[b * rows : (b + 1) * rows]
    pieces_of = lambda ref: lambda b: ref[b]
    copies = []
    for k, piece, factor in (
        (0, pieces_of(own_ref), near),
        (2, pieces_of(far_ref), far),
        (3, packed(third_ref), far),
        (1, packed(near_ref), near),
    ):
        number, cols = place(y, k, width)
        for b in range(pieces):
            at = slice(b * BLOCK, (b + 1) * BLOCK)
            grad = piece(b) * factor
            moment_next = MU * moment_ref[k, :, at] + grad
            outer_next = outer_ref[k, :, at] - LR * (MU * moment_next + grad)
            moment_buf[k, :, at] = moment_next
            outer_buf[k, :, at] = outer_next
            merged_buf[k, :, at] = (
                MIX * local_ref[k, :, at].astype(jnp.float32) + (1.0 - MIX) * outer_next
            ).astype(jnp.bfloat16)
        copies += [
            pltpu.make_async_copy(moment_buf.at[k], new_moment.at[number, :, cols], sems.at[0, k]),
            pltpu.make_async_copy(outer_buf.at[k], new_outer.at[number, :, cols], sems.at[1, k]),
            pltpu.make_async_copy(merged_buf.at[k], merged.at[0, number, :, cols], sems.at[2, k]),
        ]
        for copy in copies[-3:]:
            copy.start()
    for copy in copies:
        copy.wait()


def update(means, outer_sel, local_sel, moment_sel, workers, entries):
    _, rows, width = outer_sel.shape
    cols = QUARTERS * width // SYNCED
    return pl.pallas_call(
        lambda *refs: update_kernel(workers, entries, *refs),
        out_shape=(
            jax.ShapeDtypeStruct((SYNCED, rows, cols), jnp.float32),
            jax.ShapeDtypeStruct((SYNCED, rows, cols), jnp.float32),
            jax.ShapeDtypeStruct((1, SYNCED, rows, cols), local_sel.dtype),
        ),
        in_specs=[VMEM] * (len(means) + 3),
        out_specs=(HBM,) * 3,
        scratch_shapes=[
            pltpu.VMEM(outer_sel.shape, jnp.float32),
            pltpu.VMEM(outer_sel.shape, jnp.float32),
            pltpu.VMEM(local_sel.shape, local_sel.dtype),
            pltpu.SemaphoreType.DMA((3, QUARTERS)),
        ],
        compiler_params=PARAMS,
        name="update",
    )(*means, outer_sel, local_sel, moment_sel)


def shards(local, outer, moment, plan):
    _, frags, rows, cols = local.shape
    workers = lax.axis_size("replica")
    shares = lax.axis_size("mp")
    entries = rows * cols * shares
    inner = workers // QUARTERS
    groups = [list(range(g * inner, (g + 1) * inner)) for g in range(QUARTERS)]

    def along_y(array, k):
        return lax.ppermute(array, "replica", [(r, r ^ (k * inner)) for r in range(workers)])

    def inside(array):
        return lax.all_to_all(array, "replica", 0, 0, axis_index_groups=groups, tiled=True)

    sent = encode(plan, local, outer, workers)
    arrived = [along_y(array, k) for k, array in zip(SENT, sent)]
    own, outer_sel, local_sel, moment_sel = select(plan, local, outer, moment, workers)
    mine = add([own] + arrived)
    raw = inside(mean(inside(mine), workers))
    own_squares, quarter = squares(raw)
    far = along_y(raw, 2)
    swaps = [lax.ppermute(own_squares, "mp", [(m, m ^ bit) for m in range(shares)]) for bit in (1, 3, 2)]
    packed, total = pack(swaps, far, own_squares, quarter)
    third, near, far_total = along_y(packed, 3), along_y(packed, 1), along_y(total, 2)
    return update((quarter, total, far, far_total, third, near), outer_sel, local_sel, moment_sel, workers, entries)


def solution(mesh):
    return jax.shard_map(
        shards,
        mesh=mesh,
        in_specs=(P("replica", None, None, "mp"), P(None, None, "mp"), P(None, None, "mp"), P()),
        out_specs=(P(None, None, "mp"), P(None, None, "mp"), P("replica", None, None, "mp")),
        check_vma=False,
    )
```

```python
import jax
import jax.numpy as jnp
from jax import lax
from jax.experimental import pallas as pl
from jax.experimental.pallas import tpu as pltpu
from jax.sharding import PartitionSpec as P

SYNCED = 2
BLOCK = 128
EPS = 1e-06
CLIP = 0.2
MU = 0.9
LR = 0.7
MIX = 0.5

QUARTERS = 4
SCOPED = 32 * 1024 * 1024
HBM = pl.BlockSpec(memory_space=pltpu.HBM)
VMEM = pl.BlockSpec(memory_space=pltpu.VMEM)
PARAMS = pltpu.CompilerParams(vmem_limit_bytes=SCOPED)


SENT = (2, 3, 1)
HELD = (0, 1, 3, 2)


def in_hbm(*arrays):
    return [pltpu.with_memory_space_constraint(array, pltpu.HBM) for array in arrays]


def my_y(workers):
    return lax.axis_index("replica") // (workers // QUARTERS)


def place(y, k, width):
    quarter = jnp.bitwise_xor(y, k)
    per_fragment = QUARTERS // SYNCED
    return quarter // per_fragment, pl.ds(pl.multiple_of((quarter % per_fragment) * width, width), width)


def coded(outer, local):
    diff = outer - local.astype(jnp.float32)
    scale = jnp.max(jnp.abs(diff), axis=-1, keepdims=True) + EPS
    return (diff / scale).astype(jnp.bfloat16).astype(jnp.float32) * scale


def encode_kernel(workers, plan_hbm, local_hbm, outer_hbm, *refs):
    out_refs, (outer_ref, local_ref, plan_ref, plan_sem, sems) = refs[: len(SENT)], refs[len(SENT) :]
    width = out_refs[0].shape[0] * BLOCK
    frags = outer_ref.shape[0]
    plan_copy = pltpu.make_async_copy(plan_hbm, plan_ref, plan_sem)
    plan_copy.start()
    def copies(f):
        return (
            pltpu.make_async_copy(outer_hbm.at[f], outer_ref.at[f], sems.at[0, f]),
            pltpu.make_async_copy(local_hbm.at[0, f], local_ref.at[f], sems.at[1, f]),
        )

    for f in range(frags):
        for copy in copies(f):
            copy.start()
    y = my_y(workers)
    plan_copy.wait()
    for f in range(frags):
        for copy in copies(f):
            copy.wait()
    for k, out_ref in zip(SENT, out_refs):
        number, cols = place(y, k, width)
        f = plan_ref[number]
        for b in range(width // BLOCK):
            at = pl.ds(pl.multiple_of(cols.start + b * BLOCK, BLOCK), BLOCK)
            out_ref[b] = coded(outer_ref[f, :, at], local_ref[f, :, at])


def encode(plan, local, outer, workers):
    _, frags, rows, cols = local.shape
    width = SYNCED * cols // QUARTERS
    piece = jax.ShapeDtypeStruct((width // BLOCK, rows, BLOCK), jnp.float32)
    return pl.pallas_call(
        lambda *refs: encode_kernel(workers, *refs),
        out_shape=(piece,) * len(SENT),
        in_specs=[HBM] * 3,
        out_specs=(VMEM,) * len(SENT),
        scratch_shapes=[
            pltpu.VMEM(outer.shape, outer.dtype),
            pltpu.VMEM(local.shape[1:], local.dtype),
            pltpu.SMEM(plan.shape, jnp.int32),
            pltpu.SemaphoreType.DMA(()),
            pltpu.SemaphoreType.DMA((2, frags)),
        ],
        compiler_params=PARAMS,
        name="encode",
    )(*in_hbm(plan, local, outer))


def select_kernel(workers, plan_hbm, local_hbm, outer_hbm, moment_hbm, own_ref, outer_ref, local_ref, moment_ref, plan_ref, plan_sem, sems):
    width = outer_ref.shape[-1]
    plan_copy = pltpu.make_async_copy(plan_hbm, plan_ref, plan_sem)
    plan_copy.start()
    y = my_y(workers)
    plan_copy.wait()
    copies = []
    for k in range(QUARTERS):
        number, cols = place(y, k, width)
        f = plan_ref[number]
        copies += [
            pltpu.make_async_copy(outer_hbm.at[f, :, cols], outer_ref.at[k], sems.at[0, k]),
            pltpu.make_async_copy(local_hbm.at[0, f, :, cols], local_ref.at[k], sems.at[1, k]),
            pltpu.make_async_copy(moment_hbm.at[f, :, cols], moment_ref.at[k], sems.at[2, k]),
        ]
    for copy in copies:
        copy.start()
    for copy in copies:
        copy.wait()
    for b in range(width // BLOCK):
        at = slice(b * BLOCK, (b + 1) * BLOCK)
        own_ref[b] = coded(outer_ref[0, :, at], local_ref[0, :, at])


def select(plan, local, outer, moment, workers):
    _, frags, rows, cols = local.shape
    width = SYNCED * cols // QUARTERS
    kept = lambda dtype: jax.ShapeDtypeStruct((QUARTERS, rows, width), dtype)
    return pl.pallas_call(
        lambda *refs: select_kernel(workers, *refs),
        out_shape=(
            jax.ShapeDtypeStruct((width // BLOCK, rows, BLOCK), jnp.float32),
            kept(outer.dtype),
            kept(local.dtype),
            kept(moment.dtype),
        ),
        in_specs=[HBM] * 4,
        out_specs=(VMEM,) * 4,
        scratch_shapes=[
            pltpu.SMEM(plan.shape, jnp.int32),
            pltpu.SemaphoreType.DMA(()),
            pltpu.SemaphoreType.DMA((3, QUARTERS)),
        ],
        compiler_params=PARAMS,
        cost_estimate=pl.CostEstimate(flops=10**6, bytes_accessed=4 * 10**6, transcendentals=0),
        name="select",
    )(*in_hbm(plan, local, outer, moment))


def add_kernel(*refs):
    *parts, out_ref = refs
    out_ref[...] = (parts[0][...] + parts[1][...]) + (parts[2][...] + parts[3][...])


def add(parts):
    return pl.pallas_call(
        add_kernel,
        out_shape=jax.ShapeDtypeStruct(parts[0].shape, jnp.float32),
        in_specs=[VMEM] * QUARTERS,
        out_specs=VMEM,
        compiler_params=PARAMS,
        name="add",
    )(*parts)


def mean_kernel(workers, parts_ref, out_ref):
    total = jnp.sum(parts_ref[...], axis=0) / workers
    out_ref[...] = jnp.broadcast_to(total[None], out_ref.shape)


def mean(parts, workers):
    return pl.pallas_call(
        lambda *refs: mean_kernel(workers, *refs),
        out_shape=jax.ShapeDtypeStruct(parts.shape, jnp.float32),
        in_specs=[VMEM],
        out_specs=VMEM,
        compiler_params=PARAMS,
        name="mean",
    )(parts)


def tile_of(y, own, other):
    row = lax.broadcasted_iota(jnp.int32, (8, BLOCK), 0)
    number, _ = place(y, 0, BLOCK)
    return jnp.where(row == number, own, jnp.where(row == SYNCED - 1 - number, other, 0.0))


def first_squares_kernel(workers, own_ref, third_ref, far_ref, out_ref):
    own, third, far = [jnp.sum(ref[...] * ref[...]) for ref in (own_ref, third_ref, far_ref)]
    out_ref[...] = tile_of(my_y(workers), own, far + third)


def last_squares_kernel(workers, near_ref, first_ref, out_ref):
    near = jnp.sum(near_ref[...] * near_ref[...])
    out_ref[...] = first_ref[...] + tile_of(my_y(workers), near, 0.0)


def squares(quarters, workers):
    own, near, third, far = quarters

    def call(kernel, *operands):
        return pl.pallas_call(
            lambda *refs: kernel(workers, *refs),
            out_shape=jax.ShapeDtypeStruct((8, BLOCK), jnp.float32),
            in_specs=[VMEM] * len(operands),
            out_specs=VMEM,
            compiler_params=PARAMS,
            name="squares",
        )(*operands)

    return call(last_squares_kernel, near, call(first_squares_kernel, own, third, far))


def update_kernel(workers, entries, *refs):
    quarters, refs = refs[:QUARTERS], refs[QUARTERS:]
    squares_ref, outer_ref, local_ref, moment_ref, new_outer, new_moment, merged, outer_buf, moment_buf, merged_buf, factor_ref, sems = refs
    width = outer_ref.shape[-1]
    y = my_y(workers)
    factor_ref[...] = jnp.minimum(1.0, CLIP / jnp.sqrt(squares_ref[...] / entries + EPS))
    copies = []
    for quarter_ref, k in zip(quarters, HELD):
        number, cols = place(y, k, width)
        factor = factor_ref[pl.ds(number, 1)]
        for b in range(width // BLOCK):
            at = slice(b * BLOCK, (b + 1) * BLOCK)
            grad = quarter_ref[b] * factor
            moment_next = MU * moment_ref[k, :, at] + grad
            outer_next = outer_ref[k, :, at] - LR * (MU * moment_next + grad)
            moment_buf[k, :, at] = moment_next
            outer_buf[k, :, at] = outer_next
            merged_buf[k, :, at] = (
                MIX * local_ref[k, :, at].astype(jnp.float32) + (1.0 - MIX) * outer_next
            ).astype(jnp.bfloat16)
        copies += [
            pltpu.make_async_copy(moment_buf.at[k], new_moment.at[number, :, cols], sems.at[0, k]),
            pltpu.make_async_copy(outer_buf.at[k], new_outer.at[number, :, cols], sems.at[1, k]),
            pltpu.make_async_copy(merged_buf.at[k], merged.at[0, number, :, cols], sems.at[2, k]),
        ]
        for copy in copies[-3:]:
            copy.start()
    for copy in copies:
        copy.wait()


def update(quarters, squares_sum, outer_sel, local_sel, moment_sel, workers, entries):
    _, rows, width = outer_sel.shape
    cols = QUARTERS * width // SYNCED
    return pl.pallas_call(
        lambda *refs: update_kernel(workers, entries, *refs),
        out_shape=(
            jax.ShapeDtypeStruct((SYNCED, rows, cols), jnp.float32),
            jax.ShapeDtypeStruct((SYNCED, rows, cols), jnp.float32),
            jax.ShapeDtypeStruct((1, SYNCED, rows, cols), local_sel.dtype),
        ),
        in_specs=[VMEM] * (QUARTERS + 4),
        out_specs=(HBM,) * 3,
        scratch_shapes=[
            pltpu.VMEM(outer_sel.shape, jnp.float32),
            pltpu.VMEM(outer_sel.shape, jnp.float32),
            pltpu.VMEM(local_sel.shape, local_sel.dtype),
            pltpu.VMEM((8, BLOCK), jnp.float32),
            pltpu.SemaphoreType.DMA((3, QUARTERS)),
        ],
        compiler_params=PARAMS,
        name="update",
    )(*quarters, squares_sum, outer_sel, local_sel, moment_sel)


def shards(local, outer, moment, plan):
    _, frags, rows, cols = local.shape
    workers = lax.axis_size("replica")
    shares = lax.axis_size("mp")
    entries = rows * cols * shares
    inner = workers // QUARTERS
    groups = [list(range(g * inner, (g + 1) * inner)) for g in range(QUARTERS)]

    def along_y(array, k):
        return lax.ppermute(array, "replica", [(r, r ^ (k * inner)) for r in range(workers)])

    def inside(array):
        return lax.all_to_all(array, "replica", 0, 0, axis_index_groups=groups, tiled=True)

    sent = encode(plan, local, outer, workers)
    arrived = [along_y(array, k) for k, array in zip(SENT, sent)]
    own, outer_sel, local_sel, moment_sel = select(plan, local, outer, moment, workers)
    mine = add([own] + arrived)
    quarter = inside(mean(inside(mine), workers))
    received = {k: along_y(quarter, k) for k in SENT}
    quarters = [quarter] + [received[k] for k in HELD[1:]]
    return update(quarters, mp_total(squares(quarters, workers)), outer_sel, local_sel, moment_sel, workers, entries)


def mp_total(mine):
    swap = {bit: lax.ppermute(mine, "mp", [(m, m ^ bit) for m in range(4)]) for bit in (2, 3, 1)}
    return (mine + swap[1]) + (swap[3] + swap[2])


def solution(mesh):
    return jax.shard_map(
        shards,
        mesh=mesh,
        in_specs=(P("replica", None, None, "mp"), P(None, None, "mp"), P(None, None, "mp"), P()),
        out_specs=(P(None, None, "mp"), P(None, None, "mp"), P("replica", None, None, "mp")),
        check_vma=False,
    )
```
